256 devices in a mesh: dp: 32 (over z_hi, x, core), fsdp: 8 (over y, z_lo).
Axes of the slice: x: 4, y: 4, z: 8 (z_hi: 4, z_lo: 2; z = z_hi * 2 + z_lo), core: 2. Of those that a mesh axis runs over, the one named last changes fastest.
Arguments:
- frames_in: bfloat16 [98304, 1536], P(('dp', 'fsdp')), may hold values from -6 to 6
- dest: int32 [98304], P(('dp', 'fsdp')), may hold values from 0 to 3071, as said below
- segment: int32 [32, 3072], P('dp', 'fsdp'), may hold values from 0 to 11, never falling along the last dimension, each value on 1 to 576 neighbouring positions
- gain_in: float32 [1536], replicated, may hold values from 0.5 to 1.5
- w_glu: bfloat16 [1536, 3072], P('fsdp'), may hold values from -0.15625 to 0.15625
- kernel: float32 [31, 1536], replicated, may hold values from -1 to 1
- gain_mid: float32 [1536], replicated, may hold values from 0.5 to 1.5
- cotangent: bfloat16 [98304, 1536], P(('dp', 'fsdp')), may hold values from -6 to 6
Outputs:
- output: bfloat16 [98304, 1536], P(('dp', 'fsdp'))
- grad_frames: bfloat16 [98304, 1536], P(('dp', 'fsdp'))
- grad_weight: float32 [1536, 3072], P('fsdp')
- grad_gain_in: float32 [1536], replicated
- grad_kernel: float32 [31, 1536], replicated
- grad_gain_mid: float32 [1536], replicated
The draws below stay inside these ranges and needn't reach their ends.
Inputs may be any that keep to these rules, and one draw needn't show every extreme that they name: Within each dp index's 3072 rows, dest is a permutation of 0 to 3071, and the 384 rows of each device name exactly 48 positions in each range of 384 positions k * 384 to (k + 1) * 384 - 1.
All inputs are finite; a program needn't handle non-finite values.
Results may differ from the reference program's by a relative error of at most 0.0065.
Values may be sent and summed in bfloat16 or wider, within the bound.
A program may use at most 128 MiB of HBM per device.

```python
import math
import jax
import jax.numpy as jnp
import numpy as np
from jax import lax

D = 1536
TAPS = 31
TOK_DEV = 384
GROUP_ROWS = 3072
TOKENS = 98304
UTTERANCES = 12
UTT_MOST = 576
N_DP = 32
N_FSDP = 8


def draw_dest(key, part):
    key = jax.random.fold_in(key, 11)
    block = TOK_DEV // N_FSDP

    def one_group(group_key):
        slot_key, row_key = jax.random.split(group_key)
        sigmas = jax.vmap(lambda k: jax.random.permutation(k, TOK_DEV))(jax.random.split(slot_key, N_FSDP))
        inverse = jnp.argsort(sigmas, axis=1).astype(jnp.int32)
        taus = jax.vmap(lambda k: jax.random.permutation(k, TOK_DEV))(jax.random.split(row_key, N_FSDP))
        column = jnp.arange(TOK_DEV, dtype=jnp.int32)
        target_dev = column // block
        within = column % block
        source = jnp.arange(N_FSDP, dtype=jnp.int32)[:, None]
        target = target_dev[None, :] * TOK_DEV + inverse[target_dev[None, :], source * block + within[None, :]]
        placed = jnp.zeros((N_FSDP, TOK_DEV), jnp.int32).at[source, taus].set(target)
        return placed.reshape(-1)
    return jax.vmap(one_group)(jax.random.split(key, N_DP)).reshape(-1).astype(jnp.int32)


def block_scale(key, shape, cuts, smallest, high):
    gain = 1.0
    for dim, blocks in cuts:
        draws = jax.random.uniform(jax.random.fold_in(jax.random.fold_in(key, 6), dim), (blocks,), jnp.float32, smallest / len(cuts), high / len(cuts))
        gain = gain * jnp.repeat(jnp.exp(draws), shape[dim] // blocks).reshape((-1,) + (1,) * (len(shape) - 1 - dim))
    return gain


def split_up(count, total, limit, skew):
    weights = [(1 << 20) // math.isqrt(rank ** skew) + 1 for rank in range(2, count + 1)]
    rest, counts = total - limit - (count - 1), [1] * (count - 1)
    while rest > 0:
        movable = [i for i in range(count - 1) if counts[i] < limit]
        pool, remaining = sum([weights[i] for i in movable]), rest
        for i in movable:
            more = min(limit - counts[i], max(1, remaining * weights[i] // pool), rest)
            counts[i] = counts[i] + more
            rest = rest - more
    return np.array([limit] + counts)


def uneven_parts(own_key, number_of, total, reach, slope):
    if number_of == 2:
        one = jax.random.randint(own_key, (), max(1, total - reach), min(reach, total - 1) + 1)
        return jnp.stack([one, total - one])
    tallies = jnp.asarray(split_up(number_of, total, reach, slope), jnp.int32)
    pairs = (number_of - 1) // 2
    donor, sink = tallies[1:1 + 2 * pairs:2], tallies[2:2 + 2 * pairs:2]
    margin = jnp.minimum(donor - 1, reach - sink)
    shifted = jax.random.randint(jax.random.fold_in(own_key, 1), (pairs,), 0, 1 << 20) % (margin + 1)
    tallies = tallies.at[1:1 + 2 * pairs:2].set(donor - shifted).at[2:2 + 2 * pairs:2].set(sink + shifted)
    return tallies[jax.random.permutation(jax.random.fold_in(own_key, 2), number_of)]


def scatter_about(stream_key, shape, scale, bound, cuts=(), kind=jnp.bfloat16):
    level = block_scale(stream_key, shape, cuts, -0.22, 0.18) if cuts else 1.0
    result = jax.random.normal(stream_key, shape, jnp.float32) * scale * level
    return jnp.minimum(jnp.maximum(result, -bound), bound).astype(kind)


def setup_inputs(seed: int = 0) -> dict:
    splits = jax.random.split(jax.random.key(seed), 9)
    frames_in = scatter_about(splits[0], (TOKENS, D), 1.0, 6.0, ((0, 256),))
    dest = draw_dest(jax.random.fold_in(splits[8], 71), 0)
    segment = jax.vmap(lambda own: jnp.searchsorted(jnp.cumsum(uneven_parts(own, UTTERANCES, GROUP_ROWS, UTT_MOST, 1)), jnp.arange(GROUP_ROWS), side="right"))(jax.random.split(splits[2], N_DP)).reshape((N_DP, GROUP_ROWS)).astype(jnp.int32)
    gain_in = jnp.clip(1.0 + 0.1 * jax.random.normal(splits[3], (D,), jnp.float32), 0.5, 1.5)
    w_glu = scatter_about(splits[4], (D, 2 * D), D ** -0.5, 0.15625, ((0, 8),))
    kernel = scatter_about(splits[5], (TAPS, D), TAPS ** -0.5, 1.0, (), jnp.float32)
    gain_mid = jnp.clip(1.0 + 0.1 * jax.random.normal(splits[6], (D,), jnp.float32), 0.5, 1.5)
    cotangent = scatter_about(splits[7], (TOKENS, D), 1.0, 6.0, ((0, 256),))
    return dict(frames_in=frames_in, dest=dest, segment=segment, gain_in=gain_in, w_glu=w_glu, kernel=kernel, gain_mid=gain_mid, cotangent=cotangent)


EPS = 1e-05

def norm_rows(values):
    centre = values - lax.optimization_barrier(jnp.mean(values, axis=-1, keepdims=True))
    scale = lax.rsqrt(lax.optimization_barrier(jnp.mean(centre * centre, axis=-1, keepdims=True)) + EPS)
    return (centre * scale, scale)

def norm_back(upstream, unit, scale):
    return scale * (upstream - lax.optimization_barrier(jnp.mean(upstream, axis=-1, keepdims=True)) - unit * lax.optimization_barrier(jnp.mean(upstream * unit, axis=-1, keepdims=True)))

def tap_masks(seg_ext, seg_own, taps):
    width = seg_own.shape[0]
    return jnp.stack([seg_ext[j:j + width] == seg_own for j in range(taps)], axis=1).astype(jnp.float32)

def depthwise(extended, masks, kernel):
    width = masks.shape[0]
    total = jnp.zeros((width, extended.shape[1]), jnp.float32)
    for j in range(kernel.shape[0]):
        total = total + extended[j:j + width].astype(jnp.float32) * masks[:, j:j + 1] * kernel[j]
    return total

def kernel_grad(extended, masks, upstream):
    width = masks.shape[0]
    return jnp.stack([lax.optimization_barrier(jnp.sum(upstream * extended[j:j + width].astype(jnp.float32) * masks[:, j:j + 1], axis=0)) for j in range(masks.shape[1])], axis=0)

def one_group(frames, where, seg, cot, gain_in, w_glu, kernel, gain_mid):
    rows = seg.shape[0]
    width = w_glu.shape[0]
    taps = kernel.shape[0]
    half = (taps - 1) // 2
    packed = jnp.zeros((rows, width), jnp.bfloat16).at[where].set(frames)
    unit_in, scale_in = norm_rows(packed.astype(jnp.float32))
    normed = (unit_in * gain_in).astype(jnp.bfloat16)
    proj = jnp.dot(normed, w_glu, preferred_element_type=jnp.float32)
    value = proj[:, :width]
    sig = jax.nn.sigmoid(proj[:, width:])
    glu = (value * sig).astype(jnp.bfloat16)
    seg_ext = jnp.pad(seg, (half, half), constant_values=-1)
    masks = tap_masks(seg_ext, seg, taps)
    glu_ext = jnp.pad(glu, ((half, half), (0, 0)))
    mixed = depthwise(glu_ext, masks, kernel)
    unit_mid, scale_mid = norm_rows(mixed)
    mid = unit_mid * gain_mid
    sig_mid = jax.nn.sigmoid(mid)
    output = (packed.astype(jnp.float32) + mid * sig_mid).astype(jnp.bfloat16)
    cot_full = cot.astype(jnp.float32)
    d_mid = cot_full * (sig_mid + mid * sig_mid * (1.0 - sig_mid))
    g_gain_mid = lax.optimization_barrier(jnp.sum(d_mid * unit_mid, axis=0))
    d_mixed = norm_back(d_mid * gain_mid, unit_mid, scale_mid)
    dm_ext = jnp.pad(d_mixed, ((half, half), (0, 0)))
    d_glu = depthwise(dm_ext, masks, kernel[::-1])
    g_kernel = kernel_grad(glu_ext, masks, d_mixed)
    d_proj = jnp.concatenate([d_glu * sig, d_glu * value * sig * (1.0 - sig)], axis=1).astype(jnp.bfloat16)
    g_weight = jnp.dot(normed.T, d_proj, preferred_element_type=jnp.float32)
    d_normed = jnp.dot(d_proj, w_glu.T, preferred_element_type=jnp.float32)
    g_gain_in = lax.optimization_barrier(jnp.sum(d_normed * unit_in, axis=0))
    grad_frames = (cot_full + norm_back(d_normed * gain_in, unit_in, scale_in)).astype(jnp.bfloat16)
    return (output, grad_frames, g_weight, g_gain_in, g_kernel, g_gain_mid)

def reference(frames_in, dest, segment, gain_in, w_glu, kernel, gain_mid, cotangent):
    rows = N_FSDP * TOK_DEV
    width = w_glu.shape[0]

    def step(carry, pieces):
        frames, where, seg, cot = pieces
        output, grad_frames, g_weight, g_gain_in, g_kernel, g_gain_mid = one_group(frames, where, seg, cot, gain_in, w_glu, kernel, gain_mid)
        carry = (carry[0] + g_weight, carry[1] + g_gain_in, carry[2] + g_kernel, carry[3] + g_gain_mid)
        return (carry, (output, grad_frames))
    start = (jnp.zeros(w_glu.shape, jnp.float32), jnp.zeros(gain_in.shape, jnp.float32), jnp.zeros(kernel.shape, jnp.float32), jnp.zeros(gain_mid.shape, jnp.float32))
    sums, (outs, grads) = lax.scan(step, start, (frames_in.reshape(N_DP, rows, width), dest.reshape(N_DP, rows), segment, cotangent.reshape(N_DP, rows, width)))
    return (outs.reshape(-1, width), grads.reshape(-1, width), sums[0], sums[1], sums[2], sums[3])
```

```python
import jax
import jax.numpy as jnp
from jax import lax
from jax.experimental import pallas as pl
from jax.experimental.pallas import tpu as pltpu
from jax.sharding import PartitionSpec as P

EPS = 1e-05
ROWS = 384
D = 1536
TAPS = 31
MESH = pl.DeviceIdType.MESH
F32 = jnp.float32
BF16 = jnp.bfloat16
VMEM_LIMIT = 56 * 1024 * 1024


def place():
    dp = lax.axis_index("dp")
    me = lax.axis_index("fsdp")
    z_hi = lax.div(dp, 8)
    x = lax.rem(lax.div(dp, 2), 4)
    core = lax.rem(dp, 2)
    return dp, me, z_hi, x, core, lax.div(me, 2), lax.rem(me, 2)


def send(src, dst, send_sem, recv_sem, target):
    copy = pltpu.make_async_remote_copy(
        src_ref=src, dst_ref=dst, send_sem=send_sem, recv_sem=recv_sem, device_id=target, device_id_type=MESH
    )
    copy.start()
    return copy


def greet(targets):
    barrier = pltpu.get_barrier_semaphore()
    for target in targets:
        pl.semaphore_signal(barrier, inc=1, device_id=target, device_id_type=MESH)
    pl.semaphore_wait(barrier, len(targets))


def vec_mean(v):
    return jnp.sum(v, axis=-1, keepdims=True) * (1.0 / D)


def front_kernel(
    frames, dest, seg, w, gain, cot,
    packed, normed_t, w_out, value, sig, gext, cext, sext,
    w_all, out_buf, in_buf, normed, a_s, a_r, y_s, y_r, z_s, z_r, b_s, b_r, h_s, h_r, l_s,
):
    dp, me, z_hi, x, core, y, z_lo = place()
    sib = (dp + 1 - 2 * core, me)
    up = (lax.rem(z_hi + z_lo, 4) * 8 + x * 2 + core, me + 1 - 2 * z_lo)
    down = (lax.rem(z_hi + 3 + z_lo, 4) * 8 + x * 2 + core, me + 1 - 2 * z_lo)
    far = (lax.rem(z_hi + 3 + 2 * z_lo, 4) * 8 + x * 2 + core, me + 1 - 2 * z_lo)
    nxt = (dp, lax.rem(me + 1, 8))
    prv = (dp, lax.rem(me + 7, 8))

    greet([(dp, lax.rem(me + s, 8)) for s in range(1, 8)] + [far, sib])

    half = core * 96
    y_copies = []
    for s in (1, 3, 2):
        peer = (dp, 2 * lax.rem(y + s, 4) + z_lo)
        y_copies.append(
            send(
                w.at[pl.ds(half, 96), :],
                w_all.at[pl.ds(192 * me + half, 96), :],
                y_s.at[s - 1], y_r.at[s - 1], peer,
            )
        )
    z_copies = [
        send(
            w.at[pl.ds(half + 48, 48), :], w_all.at[pl.ds(192 * me + half + 48, 48), :],
            z_s.at[0, 0], z_r.at[0, 0], up,
        ),
        send(
            w.at[pl.ds(half, 48), :], w_all.at[pl.ds(192 * me + half, 48), :],
            z_s.at[1, 0], z_r.at[1, 0], down,
        ),
    ]
    sext[32:416, :] = seg[...]
    halos = [
        send(cot.at[368:384, :], cext.at[0:16, :], h_s.at[0], h_r.at[0], nxt),
        send(cot.at[0:16, :], cext.at[400:416, :], h_s.at[1], h_r.at[1], prv),
        send(sext.at[384:416, :], sext.at[0:32, :], h_s.at[2], h_r.at[2], nxt),
        send(sext.at[32:64, :], sext.at[416:448, :], h_s.at[3], h_r.at[3], prv),
    ]
    cot_copy = pltpu.make_async_copy(cot, cext.at[16:400, :], l_s.at[0])
    cot_copy.start()

    d = dest[...]
    k8 = lax.broadcasted_iota(jnp.int32, (8, ROWS), 0)
    rel = d - ROWS * k8
    hot = jnp.logical_and(rel >= 0, rel < ROWS)
    hot_f = jnp.where(hot, 1.0, 0.0).astype(F32)
    before = lax.broadcasted_iota(jnp.int32, (ROWS, ROWS), 0) < lax.broadcasted_iota(jnp.int32, (ROWS, ROWS), 1)
    rank = jnp.dot(hot_f.astype(BF16), jnp.where(before, 1.0, 0.0).astype(BF16), preferred_element_type=F32)
    order = jnp.sum(hot_f * (rank + 48.0 * k8.astype(F32)), axis=0, keepdims=True)
    slot = jnp.sum(hot_f * rel.astype(F32), axis=0, keepdims=True)
    high = jnp.floor(slot * (1.0 / 16.0))
    low = slot - 16.0 * high
    row_id = lax.broadcasted_iota(jnp.int32, (ROWS, ROWS), 0).astype(F32)
    perm = jnp.where(row_id == order, 1.0, 0.0).astype(BF16)
    tag_row = lax.broadcasted_iota(jnp.int32, (128, ROWS), 0)
    tags = jnp.where(tag_row == 0, high, jnp.where(tag_row == 1, low, 0.0)).astype(BF16)
    out_buf[:, D:] = lax.dot_general(perm, tags, (((1,), (1,)), ((), ())), preferred_element_type=F32).astype(BF16)
    for c in range(3):
        out_buf[:, 512 * c : 512 * c + 512] = jnp.dot(
            perm, frames[:, 512 * c : 512 * c + 512], preferred_element_type=F32
        ).astype(BF16)
    a_copies = []
    for s in (1, 7, 2, 6, 3, 5, 4):
        peer = lax.rem(me + s, 8)
        a_copies.append(
            send(
                out_buf.at[pl.ds(48 * peer, 48), :], in_buf.at[pl.ds(48 * me, 48), :],
                a_s.at[s - 1], a_r.at[s - 1], (dp, peer),
            )
        )
    own = pltpu.make_async_copy(out_buf.at[pl.ds(48 * me, 48), :], in_buf.at[pl.ds(48 * me, 48), :], l_s.at[1])
    own.start()
    own_w = pltpu.make_async_copy(w, w_all.at[pl.ds(192 * me, 192), :], l_s.at[2])
    own_w.start()

    b_copies = []

    def pass_on(shard, index):
        piece = w_all.at[pl.ds(192 * shard + half, 96), :]
        b_copies.append(send(piece, piece, b_s.at[index], b_r.at[index], sib))

    def y_arrived(n, s):
        y_copies[n].wait_recv()
        shard = 2 * lax.rem(y + 4 - s, 4) + z_lo
        base = 192 * shard + half
        top = w_all.at[pl.ds(base + 48, 48), :]
        low_rows = w_all.at[pl.ds(base, 48), :]
        z_copies.append(send(top, top, z_s.at[0, s], z_r.at[0, s], up))
        z_copies.append(send(low_rows, low_rows, z_s.at[1, s], z_r.at[1, s], down))
        pass_on(shard, s - 1)

    y_arrived(0, 1)
    y_arrived(1, 3)

    own.wait()
    for copy in a_copies:
        copy.wait_recv()
    tag = in_buf[:, D:].astype(F32)
    at = tag[:, 0:1] * 16.0 + tag[:, 1:2]
    col_id = lax.broadcasted_iota(jnp.int32, (ROWS, ROWS), 1).astype(F32)
    unperm = jnp.where(col_id == at, 1.0, 0.0).T.astype(BF16)
    for c in range(3):
        packed[:, 512 * c : 512 * c + 512] = jnp.dot(
            unperm, in_buf[:, 512 * c : 512 * c + 512], preferred_element_type=F32
        ).astype(BF16)

    def norm_body(i, carry):
        rows = pl.ds(pl.multiple_of(32 * i, 32), 32)
        v = packed[rows, :].astype(F32)
        centre = v - vec_mean(v)
        scale = lax.rsqrt(vec_mean(centre * centre) + EPS)
        normed[rows, :] = (centre * scale * gain[...]).astype(BF16)
        return carry

    lax.fori_loop(0, 12, norm_body, 0)
    for c in range(4):
        flipped = normed[:, 384 * c : 384 * c + 384].astype(F32).T.astype(BF16)
        for z in range(2):
            for p in range(2):
                to = 768 * p + 192 * c + 96 * z
                normed_t[to : to + 96, :] = flipped[192 * z + 96 * p : 192 * z + 96 * p + 96, :]

    y_arrived(2, 2)
    for n, t in enumerate((0, 1, 3, 2)):
        z_copies[2 * n].wait_recv()
        z_copies[2 * n + 1].wait_recv()
        pass_on(2 * lax.rem(y + 4 - t, 4) + 1 - z_lo, 3 + t)
    own_w.wait()
    for copy in b_copies:
        copy.wait_recv()
    w_copy = pltpu.make_async_copy(w_all, w_out, l_s.at[3])
    w_copy.start()

    def proj_body(i, carry):
        left = pl.ds(pl.multiple_of(256 * i, 256), 256)
        right = pl.ds(pl.multiple_of(256 * i + D, 256), 256)
        v = jnp.dot(normed[...], w_all[:, left], preferred_element_type=F32)
        g = jnp.dot(normed[...], w_all[:, right], preferred_element_type=F32)
        s = jax.nn.sigmoid(g)
        value[:, left] = v
        sig[:, left] = s
        gext[32:416, left] = (v * s).astype(BF16)
        return carry

    lax.fori_loop(0, 6, proj_body, 0)
    halos.append(send(gext.at[384:416, :], gext.at[0:32, :], h_s.at[4], h_r.at[4], nxt))
    halos.append(send(gext.at[32:64, :], gext.at[416:448, :], h_s.at[5], h_r.at[5], prv))
    cot_copy.wait()
    w_copy.wait()
    for copy in halos:
        copy.wait()
    for copy in a_copies + y_copies + z_copies + b_copies:
        copy.wait_send()


def front(frames, dest, seg, w, gain, cot):
    vm = pl.BlockSpec(memory_space=pltpu.VMEM)
    hbm = pl.BlockSpec(memory_space=pl.ANY)
    sems = pltpu.SemaphoreType.DMA
    return pl.pallas_call(
        front_kernel,
        out_shape=(
            jax.ShapeDtypeStruct((ROWS, D), BF16),
            jax.ShapeDtypeStruct((D, ROWS), BF16),
            jax.ShapeDtypeStruct((D, 2 * D), BF16),
            jax.ShapeDtypeStruct((ROWS, D), F32),
            jax.ShapeDtypeStruct((ROWS, D), F32),
            jax.ShapeDtypeStruct((448, D), BF16),
            jax.ShapeDtypeStruct((416, D), BF16),
            jax.ShapeDtypeStruct((448, 128), jnp.int32),
        ),
        in_specs=[vm] * 6,
        out_specs=(vm, vm, hbm, vm, vm, vm, vm, vm),
        scratch_shapes=[
            pltpu.VMEM((D, 2 * D), BF16),
            pltpu.VMEM((ROWS, D + 128), BF16),
            pltpu.VMEM((ROWS, D + 128), BF16),
            pltpu.VMEM((ROWS, D), BF16),
            sems((7,)), sems((7,)),
            sems((3,)), sems((3,)),
            sems((2, 4)), sems((2, 4)),
            sems((7,)), sems((7,)),
            sems((6,)), sems((6,)),
            sems((4,)),
        ],
        compiler_params=pltpu.CompilerParams(
            collective_id=0, has_side_effects=True, vmem_limit_bytes=VMEM_LIMIT
        ),
        name="front",
    )(frames, dest, seg, w, gain, cot)


def middle_kernel(
    gext, packed, cext, sext, kern, gain, value, sig,
    output, d_proj, small,
    gx, mx, kb, gk, seg,
):
    me = lax.axis_index("fsdp")
    edge = lax.broadcasted_iota(jnp.int32, (448, 128), 0) + ROWS * me - 32
    seg[...] = jnp.where(jnp.logical_and(edge >= 0, edge < 8 * ROWS), sext[...], -1)
    for l in range(12):
        gx[l] = gext[:, 128 * l : 128 * l + 128].astype(F32)
        for j in range(TAPS):
            kb[l, j] = jnp.broadcast_to(kern[j : j + 1, 128 * l : 128 * l + 128], (8, 128))
    gk[...] = jnp.zeros_like(gk)

    def uneven(first, last):
        return jnp.max(jnp.abs(seg[pl.ds(first, 1), :] - seg[pl.ds(last, 1), :])) > 0

    def conv(base, l, masked):
        total = [jnp.zeros((8, 128), F32) for _ in range(4)]
        if masked:
            here = [seg[pl.ds(base + 16 + 8 * t, 8), :] for t in range(4)]
        for j in range(TAPS):
            k = kb[l, j]
            for t in range(4):
                at = pl.ds(base + 1 + j + 8 * t, 8)
                v = gx[l, at, :]
                if masked:
                    v = jnp.where(seg[at, :] == here[t], v, 0.0)
                total[t] = total[t] + v * k
        for t in range(4):
            mx[l, pl.ds(base + 8 * t, 8), :] = total[t]

    def conv_block(b, carry):
        base = pl.multiple_of(32 * b, 32)
        mixed_up = uneven(base + 1, base + 62)

        @pl.when(mixed_up)
        def _():
            lax.fori_loop(0, 12, lambda l, c: (conv(base, l, True), c)[1], 0)

        @pl.when(jnp.logical_not(mixed_up))
        def _():
            lax.fori_loop(0, 12, lambda l, c: (conv(base, l, False), c)[1], 0)

        return carry

    lax.fori_loop(0, 13, conv_block, 0)

    def row_mean(parts):
        total = parts[0]
        for part in parts[1:]:
            total = total + part
        return jnp.sum(total, axis=-1, keepdims=True) * (1.0 / D)

    def norm_block(i, acc):
        base = pl.multiple_of(16 * i, 16)
        rows = pl.ds(base, 16)
        mixed = [mx[l, rows, :] for l in range(12)]
        mean = row_mean(mixed)
        centre = [m - mean for m in mixed]
        scale = lax.rsqrt(row_mean([c * c for c in centre]) + EPS)
        own = jnp.logical_and(i > 0, i < 25)
        acc_new = []
        e_all, unit_all = [], []
        back = pl.ds(pl.multiple_of(jnp.clip(base - 16, 0, ROWS - 16), 16), 16)
        for l in range(12):
            cols = slice(128 * l, 128 * l + 128)
            unit = centre[l] * scale
            mid = unit * gain[0:1, cols]
            s = jax.nn.sigmoid(mid)
            gated = mid * s

            @pl.when(own)
            def _():
                output[back, cols] = (packed[back, cols].astype(F32) + gated).astype(BF16)

            d_mid = cext[rows, cols].astype(F32) * (s + gated * (1.0 - s))
            du = d_mid * unit
            acc_new.append(acc[l] + jnp.where(own, du[0:8] + du[8:16], 0.0))
            e_all.append(d_mid * gain[0:1, cols])
            unit_all.append(unit)
        e_mean = row_mean(e_all)
        eu_mean = row_mean([e * u for e, u in zip(e_all, unit_all)])
        for l in range(12):
            mx[l, rows, :] = scale * (e_all[l] - e_mean - unit_all[l] * eu_mean)
        return tuple(acc_new)

    gain_acc = lax.fori_loop(0, 26, norm_block, tuple(jnp.zeros((8, 128), F32) for _ in range(12)))

    def conv_back(base, l, masked):
        total = [jnp.zeros((8, 128), F32) for _ in range(4)]
        glu = [gx[l, pl.ds(base + 32 + 8 * t, 8), :] for t in range(4)]
        if masked:
            here = [seg[pl.ds(base + 32 + 8 * t, 8), :] for t in range(4)]
        for j in range(TAPS):
            k = kb[l, TAPS - 1 - j]
            tap = None
            for t in range(4):
                v = mx[l, pl.ds(base + 1 + j + 8 * t, 8), :]
                if masked:
                    v = jnp.where(seg[pl.ds(base + 17 + j + 8 * t, 8), :] == here[t], v, 0.0)
                total[t] = total[t] + v * k
                tap = glu[t] * v if tap is None else tap + glu[t] * v
            gk[l, TAPS - 1 - j] += tap
        cols = pl.ds(pl.multiple_of(128 * l, 128), 128)
        for t in range(2):
            rows = pl.ds(base + 16 * t, 16)
            d_glu = jnp.concatenate([total[2 * t], total[2 * t + 1]], axis=0)
            s = sig[rows, cols]
            d_value = d_glu * s
            d_proj[0, rows, cols] = d_value.astype(BF16)
            d_proj[1, rows, cols] = (d_value * value[rows, cols] * (1.0 - s)).astype(BF16)

    def back_block(b, carry):
        base = pl.multiple_of(32 * b, 32)
        mixed_up = uneven(base + 17, base + 78)

        @pl.when(mixed_up)
        def _():
            lax.fori_loop(0, 12, lambda l, c: (conv_back(base, l, True), c)[1], 0)

        @pl.when(jnp.logical_not(mixed_up))
        def _():
            lax.fori_loop(0, 12, lambda l, c: (conv_back(base, l, False), c)[1], 0)

        return carry

    lax.fori_loop(0, 12, back_block, 0)
    for l in range(12):
        cols = slice(128 * l, 128 * l + 128)
        for j in range(TAPS):
            small[j : j + 1, cols] = jnp.sum(gk[l, j], axis=0, keepdims=True)
        small[TAPS : TAPS + 1, cols] = jnp.sum(gain_acc[l], axis=0, keepdims=True)


def middle(gext, packed, cext, sext, kern, gain, value, sig):
    vm = pl.BlockSpec(memory_space=pltpu.VMEM)
    return pl.pallas_call(
        middle_kernel,
        out_shape=(
            jax.ShapeDtypeStruct((ROWS, D), BF16),
            jax.ShapeDtypeStruct((2, ROWS, D), BF16),
            jax.ShapeDtypeStruct((32, D), F32),
        ),
        in_specs=[vm] * 8,
        out_specs=(vm, vm, vm),
        scratch_shapes=[
            pltpu.VMEM((12, 448, 128), F32),
            pltpu.VMEM((12, 416, 128), F32),
            pltpu.VMEM((12, TAPS, 8, 128), F32),
            pltpu.VMEM((12, TAPS, 8, 128), F32),
            pltpu.VMEM((448, 128), jnp.int32),
        ],
        compiler_params=pltpu.CompilerParams(vmem_limit_bytes=VMEM_LIMIT),
        name="middle",
    )(gext, packed, cext, sext, kern, gain, value, sig)


def back_kernel(
    normed_t, d_proj, w, packed, gain, cot, small_in,
    grad_frames, w_grad, small,
    ncat, pcat, dn, p0, p1, r0, r1, e0, e1, s0, s1, f, t_in, g, u_in, sa, sb, sy, sx, sz,
    c_s, c_r, q0_s, q0_r, q1_s, q1_r, m0_s, m0_r, m1_s, m1_r, z_s, z_r, u_s, u_r, v_s, v_r, x_s, x_r,
    k_s, k_r, ky_s, ky_r, kx_s, kx_r, kz_s, kz_r,
):
    dp, me, z_hi, x, core, y, z_lo = place()
    sib = (dp + 1 - 2 * core, me)
    pair = (dp, me + 1 - 2 * z_lo)

    def x_of(s):
        return lax.rem(x + s, 4)

    def y_of(s):
        return lax.rem(y + s, 4)

    def z_of(s):
        return lax.rem(z_hi + s, 4)

    def x_dev(s):
        return (z_hi * 8 + x_of(s) * 2 + core, me)

    def y_dev(s):
        return (dp, 2 * y_of(s) + z_lo)

    def z_dev(s):
        return (z_of(s) * 8 + x * 2 + core, me)

    steps = (1, 3, 2)
    greet(
        [sib, pair] + [x_dev(s) for s in steps] + [y_dev(s) for s in steps] + [z_dev(s) for s in steps]
    )
    sends = []

    core_copies = [
        send(normed_t, ncat.at[:, 384:768], c_s.at[0], c_r.at[0], sib),
        send(d_proj.at[1 - core], pcat.at[384:768, :], c_s.at[1], c_r.at[1], sib),
    ]
    sends += core_copies
    ncat[:, 0:384] = normed_t[...]
    pcat[0:384, :] = d_proj[core]

    def dn_body(i, carry):
        cols = pl.ds(pl.multiple_of(256 * i, 256), 256)
        dims = (((1,), (1,)), ((), ()))
        dn[:, cols] = lax.dot_general(
            d_proj[0], w[cols, 0:D], dims, preferred_element_type=F32
        ) + lax.dot_general(d_proj[1], w[cols, D : 2 * D], dims, preferred_element_type=F32)
        return carry

    lax.fori_loop(0, 6, dn_body, 0)
    for copy in core_copies:
        copy.wait_recv()

    stage0, stage1 = [], []
    for s in (1, 3, 2, 0):
        rows = pl.ds(pl.multiple_of(192 * y_of(s), 64), 192)

        def body0(i, carry, rows=rows):
            cols = pl.ds(pl.multiple_of(512 * i, 512), 512)
            p0[rows, cols] = jnp.dot(ncat[rows, :], pcat[:, cols], preferred_element_type=F32).astype(BF16)
            return carry

        lax.fori_loop(0, 3, body0, 0)
        if s:
            stage0.append(send(p0.at[rows, :], r0.at[s - 1], q0_s.at[s - 1], q0_r.at[s - 1], y_dev(s)))
        where = x_of(s)
        cols1 = pl.ds(pl.multiple_of(384 * where, 128), 384)

        def body1(i, carry, cols1=cols1, where=where):
            rows1 = pl.multiple_of(256 * i, 256)
            p1[where, pl.ds(rows1, 256), :] = jnp.dot(
                ncat[pl.ds(768 + rows1, 256), :], pcat[:, cols1], preferred_element_type=F32
            ).astype(BF16)
            return carry

        lax.fori_loop(0, 3, body1, 0)
        if s:
            stage1.append(send(p1.at[where], r1.at[s - 1], q1_s.at[s - 1], q1_r.at[s - 1], x_dev(s)))

    def frames_body(i, acc):
        rows = pl.ds(pl.multiple_of(16 * i, 16), 16)
        v = packed[rows, :].astype(F32)
        centre = v - vec_mean(v)
        scale = lax.rsqrt(vec_mean(centre * centre) + EPS)
        unit = centre * scale
        up = dn[rows, :]
        du = up * unit
        e = up * gain[...]
        back = scale * (e - vec_mean(e) - unit * vec_mean(e * unit))
        grad_frames[rows, :] = (cot[rows, :].astype(F32) + back).astype(BF16)
        return acc + du[0:8, :] + du[8:16, :]

    gain_acc = lax.fori_loop(0, 24, frames_body, jnp.zeros((8, D), F32))

    sa[0:32, :] = small_in[...]
    sa[32:40, :] = jnp.where(
        lax.broadcasted_iota(jnp.int32, (8, D), 0) == 0, jnp.sum(gain_acc, axis=0, keepdims=True), 0.0
    )
    mine = pl.multiple_of(768 * core, 128)
    other = pl.multiple_of(768 - 768 * core, 128)
    copy = send(sa.at[:, pl.ds(other, 768)], sb.at[:, 0:768], k_s.at[0], k_r.at[0], sib)
    sends.append(copy)
    copy.wait_recv()
    sb[:, 768:1536] = sb[:, 0:768] + sa[:, pl.ds(mine, 768)]
    z_mine = pl.multiple_of(768 + 384 * z_lo, 128)
    z_other = pl.multiple_of(768 + 384 - 384 * z_lo, 128)
    copy = send(sb.at[:, pl.ds(z_other, 384)], sy.at[4], k_s.at[1], k_r.at[1], pair)
    sends.append(copy)
    copy.wait_recv()
    sy[pl.ds(y, 1)] = (sb[:, pl.ds(z_mine, 384)] + sy[4])[None]
    y_small = [send(sy.at[y], sy.at[y], ky_s.at[s - 1], ky_r.at[s - 1], y_dev(s)) for s in steps]
    sends += y_small

    for copy in stage0:
        copy.wait_recv()
    rows = pl.ds(pl.multiple_of(192 * y, 64), 192)
    for c in range(3):
        cols = slice(512 * c, 512 * c + 512)
        e0[:, cols] = (
            p0[rows, cols].astype(F32) + r0[0, :, cols].astype(F32) + r0[1, :, cols].astype(F32) + r0[2, :, cols].astype(F32)
        ).astype(BF16)
    second0 = [
        send(
            e0.at[:, pl.ds(pl.multiple_of(384 * x_of(s), 128), 384)], s0.at[s - 1],
            m0_s.at[s - 1], m0_r.at[s - 1], x_dev(s),
        )
        for s in steps
    ]
    for copy in stage1:
        copy.wait_recv()
    for c in range(3):
        rows_c = slice(256 * c, 256 * c + 256)
        e1[rows_c, :] = (
            p1[x, rows_c, :].astype(F32) + r1[0, rows_c, :].astype(F32) + r1[1, rows_c, :].astype(F32) + r1[2, rows_c, :].astype(F32)
        ).astype(BF16)
    second1 = [
        send(
            e1.at[pl.ds(pl.multiple_of(192 * y_of(s), 64), 192), :], s1.at[s - 1],
            m1_s.at[s - 1], m1_r.at[s - 1], y_dev(s),
        )
        for s in steps
    ]
    for copy in y_small:
        copy.wait_recv()
    sx[pl.ds(x, 1)] = (sy[0] + sy[1] + sy[2] + sy[3])[None]
    x_small = [send(sx.at[x], sx.at[x], kx_s.at[s - 1], kx_r.at[s - 1], x_dev(s)) for s in steps]
    sends += stage0 + stage1 + second0 + second1 + x_small

    for copy in second0:
        copy.wait_recv()
    own0 = e0[:, pl.ds(pl.multiple_of(384 * x, 128), 384)].astype(F32)
    sum0 = (own0 + s0[0].astype(F32) + s0[1].astype(F32) + s0[2].astype(F32)).astype(BF16)
    f[0, 0:96, :] = sum0[0:96, :]
    f[1, 0:96, :] = sum0[96:192, :]
    for copy in second1:
        copy.wait_recv()
    own1 = e1[rows, :].astype(F32)
    sum1 = (own1 + s1[0].astype(F32) + s1[1].astype(F32) + s1[2].astype(F32)).astype(BF16)
    f[0, 96:192, :] = sum1[0:96, :]
    f[1, 96:192, :] = sum1[96:192, :]
    third = send(f.at[1 - z_lo], t_in, z_s.at[0], z_r.at[0], pair)
    sends.append(third)
    for copy in x_small:
        copy.wait_recv()
    sz[pl.ds(z_hi, 1)] = (sx[0] + sx[1] + sx[2] + sx[3])[None]
    z_small = [send(sz.at[z_hi], sz.at[z_hi], kz_s.at[s - 1], kz_r.at[s - 1], z_dev(s)) for s in steps]
    sends += z_small
    third.wait_recv()
    g[...] = (f[z_lo].astype(F32) + t_in[...].astype(F32)).astype(BF16)

    fourth = [
        send(
            g.at[pl.ds(pl.multiple_of(48 * z_of(s), 16), 48), :], u_in.at[s - 1],
            u_s.at[s - 1], u_r.at[s - 1], z_dev(s),
        )
        for s in steps
    ]
    sends += fourth
    for copy in z_small:
        copy.wait_recv()
    sb[:, 0:384] = sz[0] + sz[1] + sz[2] + sz[3]
    col_here = pl.multiple_of(768 * core + 384 * z_lo, 128)
    small[:, pl.ds(col_here, 384)] = sb[:, 0:384]
    here = small.at[:, pl.ds(col_here, 384)]
    small_z = send(here, here, k_s.at[2], k_r.at[2], pair)
    sends.append(small_z)
    for copy in fourth:
        copy.wait_recv()
    z_rows = pl.ds(pl.multiple_of(48 * z_hi, 16), 48)
    x_cols = pl.ds(pl.multiple_of(384 * x, 128), 384)
    w_grad[pl.ds(core, 1), z_rows, x_cols] = (
        g[z_rows, :].astype(F32) + u_in[0].astype(F32) + u_in[1].astype(F32) + u_in[2].astype(F32)
    ).astype(BF16)[None]
    piece = w_grad.at[core, z_rows, x_cols]
    fifth = [send(piece, piece, v_s.at[s - 1], v_r.at[s - 1], z_dev(s)) for s in steps]
    sends += fifth
    small_z.wait_recv()
    half = small.at[:, pl.ds(mine, 768)]
    small_c = send(half, half, k_s.at[3], k_r.at[3], sib)
    sends.append(small_c)
    for copy in fifth:
        copy.wait_recv()

    piece = w_grad.at[core, :, x_cols]
    sixth = [send(piece, piece, x_s.at[s - 1], x_r.at[s - 1], x_dev(s)) for s in steps]
    sends += sixth
    for copy in sixth:
        copy.wait_recv()
    last = send(w_grad.at[core], w_grad.at[core], c_s.at[2], c_r.at[2], sib)
    sends.append(last)
    small_c.wait_recv()
    last.wait_recv()
    for copy in sends:
        copy.wait_send()


def back(normed_t, d_proj, w, packed, gain, cot, small_in):
    vm = pl.BlockSpec(memory_space=pltpu.VMEM)
    sems = pltpu.SemaphoreType.DMA
    three = [sems((3,)), sems((3,))]
    return pl.pallas_call(
        back_kernel,
        out_shape=(
            jax.ShapeDtypeStruct((ROWS, D), BF16),
            jax.ShapeDtypeStruct((2, 192, D), BF16),
            jax.ShapeDtypeStruct((40, D), F32),
        ),
        in_specs=[vm] * 7,
        out_specs=(vm, vm, vm),
        scratch_shapes=[
            pltpu.VMEM((D, 768), BF16),
            pltpu.VMEM((768, D), BF16),
            pltpu.VMEM((ROWS, D), F32),
            pltpu.VMEM((768, D), BF16),
            pltpu.VMEM((4, 768, 384), BF16),
            pltpu.VMEM((3, 192, D), BF16),
            pltpu.VMEM((3, 768, 384), BF16),
            pltpu.VMEM((192, D), BF16),
            pltpu.VMEM((768, 384), BF16),
            pltpu.VMEM((3, 192, 384), BF16),
            pltpu.VMEM((3, 192, 384), BF16),
            pltpu.VMEM((2, 192, 384), BF16),
            pltpu.VMEM((192, 384), BF16),
            pltpu.VMEM((192, 384), BF16),
            pltpu.VMEM((3, 48, 384), BF16),
            pltpu.VMEM((40, D), F32),
            pltpu.VMEM((40, D), F32),
            pltpu.VMEM((5, 40, 384), F32),
            pltpu.VMEM((4, 40, 384), F32),
            pltpu.VMEM((4, 40, 384), F32),
            sems((3,)), sems((3,)),
            *three, *three, *three, *three,
            sems((1,)), sems((1,)),
            *three, *three, *three,
            sems((4,)), sems((4,)),
            *three, *three, *three,
        ],
        compiler_params=pltpu.CompilerParams(
            collective_id=1, has_side_effects=True, vmem_limit_bytes=VMEM_LIMIT
        ),
        name="back",
    )(normed_t, d_proj, w, packed, gain, cot, small_in)


def on_device(frames_in, dest, segment, gain_in, w_glu, kernel, gain_mid, cotangent):
    seg = jnp.broadcast_to(segment.reshape(ROWS, 1), (ROWS, 128))
    gain = gain_in.reshape(1, D)
    packed, normed_t, w, value, sig, gext, cext, sext = front(
        frames_in, dest.reshape(1, ROWS), seg, w_glu, gain, cotangent
    )
    output, d_proj, small_in = middle(
        gext, packed, cext, sext, kernel, gain_mid.reshape(1, D), value, sig
    )
    grad_frames, w_grad, small = back(normed_t, d_proj, w, packed, gain, cotangent, small_in)
    grad_weight = jnp.concatenate([w_grad[0], w_grad[1]], axis=1).astype(F32)
    return (output, grad_frames, grad_weight, small[32], small[:TAPS], small[TAPS])


def solution(mesh):
    return jax.shard_map(
        on_device,
        mesh=mesh,
        in_specs=(
            P(("dp", "fsdp"), None),
            P(("dp", "fsdp")),
            P("dp", "fsdp"),
            P(),
            P("fsdp", None),
            P(),
            P(),
            P(("dp", "fsdp"), None),
        ),
        out_specs=(
            P(("dp", "fsdp"), None),
            P(("dp", "fsdp"), None),
            P("fsdp", None),
            P(),
            P(),
            P(),
        ),
        check_vma=False,
    )
```

```python
import jax
import jax.numpy as jnp
from jax import lax
from jax.experimental import pallas as pl
from jax.experimental.pallas import tpu as pltpu
from jax.sharding import PartitionSpec as P

EPS = 1e-05
ROWS = 384
D = 1536
TAPS = 31
MESH = pl.DeviceIdType.MESH
F32 = jnp.float32
BF16 = jnp.bfloat16
VMEM_LIMIT = 61 * 1024 * 1024


def place():
    dp = lax.axis_index("dp")
    me = lax.axis_index("fsdp")
    z_hi = lax.div(dp, 8)
    x = lax.rem(lax.div(dp, 2), 4)
    core = lax.rem(dp, 2)
    return dp, me, z_hi, x, core, lax.div(me, 2), lax.rem(me, 2)


def send(src, dst, send_sem, recv_sem, target):
    copy = pltpu.make_async_remote_copy(
        src_ref=src, dst_ref=dst, send_sem=send_sem, recv_sem=recv_sem, device_id=target, device_id_type=MESH
    )
    copy.start()
    return copy


def greet(targets):
    barrier = pltpu.get_barrier_semaphore()
    for target in targets:
        pl.semaphore_signal(barrier, inc=1, device_id=target, device_id_type=MESH)
    pl.semaphore_wait(barrier, len(targets))


def sigmoid(v):
    return 0.5 * jnp.tanh(0.5 * v) + 0.5


def vec_mean(v):
    return jnp.sum(v, axis=-1, keepdims=True) * (1.0 / D)


def block_kernel(
    frames, dest, segment, w, gain, cot, kern, gain_m,
    output, grad_frames, w_grad, small,
    packed, value, sig, gext, cext, sext, stat,
    w_all, out_buf, in_buf, normed, gx, mx, ex, kb, gk, seg, s1, s2,
    ncat, pcat, psend, dn, p0, p1, r0, r1, e0, e1, s0_in, s1_in, f, u_in, sa, sb, sy, sx, sz,
    a_s, a_r, y_s, y_r, z_s, z_r, b_s, b_r, h_s, h_r, l_s,
    c_s, c_r, q0_s, q0_r, q1_s, q1_r, m0_s, m0_r, m1_s, m1_r, u_s, u_r, v_s, v_r, x_s, x_r, d_s, d_r,
    k_s, k_r, ky_s, ky_r, kx_s, kx_r, kz_s, kz_r,
):
    dp, me, z_hi, x, core, y, z_lo = place()
    sib = (dp + 1 - 2 * core, me)
    up = (lax.rem(z_hi + z_lo, 4) * 8 + x * 2 + core, me + 1 - 2 * z_lo)
    down = (lax.rem(z_hi + 3 + z_lo, 4) * 8 + x * 2 + core, me + 1 - 2 * z_lo)
    far = (lax.rem(z_hi + 3 + 2 * z_lo, 4) * 8 + x * 2 + core, me + 1 - 2 * z_lo)
    nxt = (dp, lax.rem(me + 1, 8))
    prv = (dp, lax.rem(me + 7, 8))

    steps = (1, 3, 2)

    def x_of(s):
        return lax.rem(x + s, 4)

    def y_of(s):
        return lax.rem(y + s, 4)

    def z_of(s):
        return lax.rem(z_hi + s, 4)

    def x_dev(s):
        return (z_hi * 8 + x_of(s) * 2 + core, me)

    def y_dev(s):
        return (dp, 2 * y_of(s) + z_lo)

    def z_dev(s, same):
        return (z_of(s) * 8 + x * 2 + core, me if same else me + 1 - 2 * z_lo)

    pair = (dp, me + 1 - 2 * z_lo)
    greet(
        [(dp, lax.rem(me + s, 8)) for s in range(1, 8)]
        + [sib]
        + [x_dev(s) for s in steps]
        + [z_dev(s, True) for s in steps]
        + [z_dev(s, False) for s in steps]
    )
    sends = []

    half = core * 96
    y_copies = []
    for s in (1, 3, 2):
        peer = (dp, 2 * lax.rem(y + s, 4) + z_lo)
        y_copies.append(
            send(
                w.at[pl.ds(half, 96), :],
                w_all.at[pl.ds(192 * me + half, 96), :],
                y_s.at[s - 1], y_r.at[s - 1], peer,
            )
        )
    z_copies = [
        send(
            w.at[pl.ds(half + 48, 48), :], w_all.at[pl.ds(192 * me + half + 48, 48), :],
            z_s.at[0, 0], z_r.at[0, 0], up,
        ),
        send(
            w.at[pl.ds(half, 48), :], w_all.at[pl.ds(192 * me + half, 48), :],
            z_s.at[1, 0], z_r.at[1, 0], down,
        ),
    ]
    sext[32:416, :] = jnp.broadcast_to(segment[...].astype(F32), (128, ROWS)).T.astype(jnp.int32)
    halos = [
        send(cot.at[368:384, :], cext.at[0:16, :], h_s.at[0], h_r.at[0], nxt),
        send(cot.at[0:16, :], cext.at[400:416, :], h_s.at[1], h_r.at[1], prv),
        send(sext.at[384:416, :], sext.at[0:32, :], h_s.at[2], h_r.at[2], nxt),
        send(sext.at[32:64, :], sext.at[416:448, :], h_s.at[3], h_r.at[3], prv),
    ]
    cot_copy = pltpu.make_async_copy(cot, cext.at[16:400, :], l_s.at[0])
    cot_copy.start()

    d = dest[...].reshape(1, ROWS)
    gain_in = gain[...].reshape(1, D)
    k8 = lax.broadcasted_iota(jnp.int32, (8, ROWS), 0)
    rel = d - ROWS * k8
    hot = jnp.logical_and(rel >= 0, rel < ROWS)
    hot_f = jnp.where(hot, 1.0, 0.0).astype(F32)
    before = lax.broadcasted_iota(jnp.int32, (ROWS, ROWS), 0) < lax.broadcasted_iota(jnp.int32, (ROWS, ROWS), 1)
    rank = jnp.dot(hot_f.astype(BF16), jnp.where(before, 1.0, 0.0).astype(BF16), preferred_element_type=F32)
    order = jnp.sum(hot_f * (rank + 48.0 * k8.astype(F32)), axis=0, keepdims=True)
    slot = jnp.sum(hot_f * rel.astype(F32), axis=0, keepdims=True)
    high = jnp.floor(slot * (1.0 / 16.0))
    low = slot - 16.0 * high
    row_id = lax.broadcasted_iota(jnp.int32, (ROWS, ROWS), 0).astype(F32)
    perm = jnp.where(row_id == order, 1.0, 0.0).astype(BF16)
    tag_row = lax.broadcasted_iota(jnp.int32, (128, ROWS), 0)
    tags = jnp.where(tag_row == 0, high, jnp.where(tag_row == 1, low, 0.0)).astype(BF16)
    out_buf[:, D:] = lax.dot_general(perm, tags, (((1,), (1,)), ((), ())), preferred_element_type=F32).astype(BF16)
    for c in range(3):
        out_buf[:, 512 * c : 512 * c + 512] = jnp.dot(
            perm, frames[:, 512 * c : 512 * c + 512], preferred_element_type=F32
        ).astype(BF16)
    a_copies = []
    for s in (1, 7, 2, 6, 3, 5, 4):
        peer = lax.rem(me + s, 8)
        a_copies.append(
            send(
                out_buf.at[pl.ds(48 * peer, 48), :], in_buf.at[pl.ds(48 * me, 48), :],
                a_s.at[s - 1], a_r.at[s - 1], (dp, peer),
            )
        )
    own = pltpu.make_async_copy(out_buf.at[pl.ds(48 * me, 48), :], in_buf.at[pl.ds(48 * me, 48), :], l_s.at[1])
    own.start()
    own_w = pltpu.make_async_copy(w, w_all.at[pl.ds(192 * me, 192), :], l_s.at[2])
    own_w.start()

    b_copies = []

    def pass_on(shard, index):
        piece = w_all.at[pl.ds(192 * shard + half, 96), :]
        b_copies.append(send(piece, piece, b_s.at[index], b_r.at[index], sib))

    def y_arrived(n, s):
        y_copies[n].wait_recv()
        shard = 2 * lax.rem(y + 4 - s, 4) + z_lo
        base = 192 * shard + half
        top = w_all.at[pl.ds(base + 48, 48), :]
        low_rows = w_all.at[pl.ds(base, 48), :]
        z_copies.append(send(top, top, z_s.at[0, s], z_r.at[0, s], up))
        z_copies.append(send(low_rows, low_rows, z_s.at[1, s], z_r.at[1, s], down))
        pass_on(shard, s - 1)

    y_arrived(0, 1)
    y_arrived(1, 3)

    own.wait()
    for copy in a_copies:
        copy.wait_recv()
    tag = in_buf[:, D:].astype(F32)
    at = tag[:, 0:1] * 16.0 + tag[:, 1:2]
    col_id = lax.broadcasted_iota(jnp.int32, (ROWS, ROWS), 1).astype(F32)
    unperm = jnp.where(col_id == at, 1.0, 0.0).T.astype(BF16)
    for c in range(3):
        packed[:, 512 * c : 512 * c + 512] = jnp.dot(
            unperm, in_buf[:, 512 * c : 512 * c + 512], preferred_element_type=F32
        ).astype(BF16)

    def norm_body(i, carry):
        rows = pl.ds(pl.multiple_of(32 * i, 32), 32)
        v = packed[rows, :].astype(F32)
        mean = vec_mean(v)
        centre = v - mean
        scale = lax.rsqrt(vec_mean(centre * centre) + EPS)
        stat[0, rows, :] = jnp.broadcast_to(mean, (32, 128))
        stat[1, rows, :] = jnp.broadcast_to(scale, (32, 128))
        normed[rows, :] = (centre * scale * gain_in).astype(BF16)
        return carry

    lax.fori_loop(0, 12, norm_body, 0)
    for c in range(4):
        flipped = normed[:, 384 * c : 384 * c + 384].astype(F32).T.astype(BF16)
        for z in range(2):
            for p in range(2):
                to = 768 * p + 192 * c + 96 * z
                ncat[to : to + 96, 0:384] = flipped[192 * z + 96 * p : 192 * z + 96 * p + 96, :]

    share = send(ncat.at[:, 0:384], ncat.at[:, 384:768], c_s.at[0], c_r.at[0], sib)
    sends.append(share)
    y_arrived(2, 2)
    for n, t in enumerate((0, 1, 3, 2)):
        z_copies[2 * n].wait_recv()
        z_copies[2 * n + 1].wait_recv()
        pass_on(2 * lax.rem(y + 4 - t, 4) + 1 - z_lo, 3 + t)
    own_w.wait()
    for copy in b_copies:
        copy.wait_recv()

    def proj_body(i, carry):
        left = pl.ds(pl.multiple_of(256 * i, 256), 256)
        right = pl.ds(pl.multiple_of(256 * i + D, 256), 256)
        v = jnp.dot(normed[...], w_all[:, left], preferred_element_type=F32)
        g = jnp.dot(normed[...], w_all[:, right], preferred_element_type=F32)
        s = sigmoid(g)
        value[:, left] = v
        sig[:, left] = s
        gext[32:416, left] = (v * s).astype(BF16)
        return carry

    lax.fori_loop(0, 6, proj_body, 0)
    halos.append(send(gext.at[384:416, :], gext.at[0:32, :], h_s.at[4], h_r.at[4], nxt))
    halos.append(send(gext.at[32:64, :], gext.at[416:448, :], h_s.at[5], h_r.at[5], prv))

    for l in range(12):
        cols = slice(128 * l, 128 * l + 128)
        gx[l, 32:416, :] = gext[32:416, cols].astype(F32)
        for j in range(TAPS):
            kb[l, j] = jnp.broadcast_to(kern[j : j + 1, cols], (8, 128))
    gk[...] = jnp.zeros_like(gk)
    s1[...] = jnp.zeros_like(s1)
    cot_copy.wait()
    for copy in halos:
        copy.wait_recv()
    for l in range(12):
        cols = slice(128 * l, 128 * l + 128)
        gx[l, 0:32, :] = gext[0:32, cols].astype(F32)
        gx[l, 416:448, :] = gext[416:448, cols].astype(F32)
    edge = lax.broadcasted_iota(jnp.int32, (448, 128), 0) + ROWS * me - 32
    seg[...] = jnp.where(jnp.logical_and(edge >= 0, edge < 8 * ROWS), sext[...], -1)

    def conv_block(n, carry):
        base = pl.multiple_of(32 * lax.div(n, 4), 32)
        l0 = 3 * lax.rem(n, 4)
        total = [[jnp.zeros((8, 128), F32) for _ in range(4)] for _ in range(3)]
        here = [seg[pl.ds(base + 16 + 8 * t, 8), :] for t in range(4)]
        for j in range(TAPS):
            taps = [kb[l0 + i, j] for i in range(3)]
            for t in range(4):
                at = pl.ds(base + 1 + j + 8 * t, 8)
                same = seg[at, :] == here[t]
                for i in range(3):
                    total[i][t] = total[i][t] + jnp.where(same, gx[l0 + i, at, :], 0.0) * taps[i]
        for t in range(4):
            at = pl.ds(base + 8 * t, 8)
            for i in range(3):
                mx[l0 + i, at, :] = total[i][t]
            s1[at, :] += total[0][t] + total[1][t] + total[2][t]
        return carry

    lax.fori_loop(0, 52, conv_block, 0)

    def lane_mean(v):
        return jnp.broadcast_to(jnp.sum(v, axis=-1, keepdims=True) * (1.0 / D), v.shape)

    def stat_block(i, carry):
        rows = pl.ds(pl.multiple_of(104 * i, 8), 104)
        mean = lane_mean(s1[rows, :])
        square = jnp.zeros((104, 128), F32)
        for l in range(12):
            centre = mx[l, rows, :] - mean
            mx[l, rows, :] = centre
            square = square + centre * centre
        s1[rows, :] = lax.rsqrt(lane_mean(square) + EPS)
        return carry

    lax.fori_loop(0, 4, stat_block, 0)
    gain_mid = gain_m[...].reshape(1, D)

    def gate_rows(base, size, own, acc):
        rows = pl.ds(base, size)
        scale = s1[rows, :]
        sum_e = jnp.zeros((size, 128), F32)
        sum_eu = jnp.zeros((size, 128), F32)
        sums = []
        for l in range(12):
            cols = slice(128 * l, 128 * l + 128)
            unit = mx[l, rows, :] * scale
            mid = unit * gain_mid[:, cols]
            s = sigmoid(mid)
            gated = mid * s
            d_mid = cext[rows, cols].astype(F32) * (s + gated * (1.0 - s))
            if own:
                to = pl.ds(base - 16, size)
                output[to, cols] = (packed[to, cols].astype(F32) + gated).astype(BF16)
                du = d_mid * unit
                part = acc[l]
                for t in range(size // 8):
                    part = part + du[8 * t : 8 * t + 8, :]
                sums.append(part)
            e = d_mid * gain_mid[:, cols]
            sum_e = sum_e + e
            sum_eu = sum_eu + e * unit
            mx[l, rows, :] = unit
            ex[l, rows, :] = e
        s2[0, rows, :] = sum_e
        s2[1, rows, :] = sum_eu
        return tuple(sums)

    gate_rows(0, 16, False, None)
    gate_rows(400, 16, False, None)
    gain_acc = lax.fori_loop(
        0, 12, lambda i, acc: gate_rows(pl.multiple_of(16 + 32 * i, 16), 32, True, acc),
        tuple(jnp.zeros((8, 128), F32) for _ in range(12)),
    )

    def mixed_block(i, carry):
        rows = pl.ds(pl.multiple_of(104 * i, 8), 104)
        e_mean = lane_mean(s2[0, rows, :])
        eu_mean = lane_mean(s2[1, rows, :])
        scale = s1[rows, :]
        for l in range(12):
            mx[l, rows, :] = scale * (ex[l, rows, :] - e_mean - mx[l, rows, :] * eu_mean)
        return carry

    lax.fori_loop(0, 4, mixed_block, 0)

    stage0, stage1 = [], []
    own_half = pl.multiple_of(D * core, 128)
    other_half = pl.multiple_of(D - D * core, 128)
    for n, s in enumerate((1, 3, 2, 0)):
        q = x_of(s)
        q0 = pl.multiple_of(384 * q, 128)
        q_cols = pl.ds(q0, 384)
        l0 = 3 * q

        def back_block(b, carry, l0=l0, q0=q0):
            base = pl.multiple_of(32 * b, 32)
            total = [[jnp.zeros((8, 128), F32) for _ in range(4)] for _ in range(3)]
            glu = [[gx[l0 + i, pl.ds(base + 32 + 8 * t, 8), :] for t in range(4)] for i in range(3)]
            here = [seg[pl.ds(base + 32 + 8 * t, 8), :] for t in range(4)]
            for j in range(TAPS):
                taps = [kb[l0 + i, TAPS - 1 - j] for i in range(3)]
                grads = [None] * 3
                for t in range(4):
                    same = seg[pl.ds(base + 17 + j + 8 * t, 8), :] == here[t]
                    at = pl.ds(base + 1 + j + 8 * t, 8)
                    for i in range(3):
                        v = jnp.where(same, mx[l0 + i, at, :], 0.0)
                        total[i][t] = total[i][t] + v * taps[i]
                        grads[i] = glu[i][t] * v if t == 0 else grads[i] + glu[i][t] * v
                for i in range(3):
                    gk[l0 + i, TAPS - 1 - j] += grads[i]
            for i in range(3):
                cols = pl.ds(pl.multiple_of(q0 + 128 * i, 128), 128)
                for t in range(2):
                    rows = pl.ds(base + 16 * t, 16)
                    d_glu = jnp.concatenate([total[i][2 * t], total[i][2 * t + 1]], axis=0)
                    sg = sig[rows, cols]
                    d_value = d_glu * sg
                    d_gate = d_value * value[rows, cols] * (1.0 - sg)
                    pcat[rows, cols] = jnp.where(core == 0, d_value, d_gate).astype(BF16)
                    psend[rows, cols] = jnp.where(core == 0, d_gate, d_value).astype(BF16)
            return carry

        lax.fori_loop(0, 12, back_block, 0)
        swap = send(psend.at[:, q_cols], pcat.at[384:768, q_cols], d_s.at[n], d_r.at[n], sib)
        sends.append(swap)
        own_cols = pl.ds(pl.multiple_of(own_half + q0, 128), 384)
        other_cols = pl.ds(pl.multiple_of(other_half + q0, 128), 384)

        def dn_body(i, carry, n=n, q_cols=q_cols, own_cols=own_cols, other_cols=other_cols):
            cols = pl.ds(pl.multiple_of(256 * i, 256), 256)
            dims = (((1,), (1,)), ((), ()))
            part = lax.dot_general(
                pcat[0:384, q_cols], w_all[cols, own_cols], dims, preferred_element_type=F32
            ) + lax.dot_general(psend[:, q_cols], w_all[cols, other_cols], dims, preferred_element_type=F32)
            dn[:, cols] = part if n == 0 else dn[:, cols] + part
            return carry

        lax.fori_loop(0, 6, dn_body, 0)
        if n == 0:
            share.wait_recv()
        swap.wait_recv()

        def body0(i, carry, q_cols=q_cols):
            rows = pl.ds(pl.multiple_of(256 * i, 256), 256)
            p0[rows, q_cols] = jnp.dot(ncat[rows, :], pcat[:, q_cols], preferred_element_type=F32).astype(BF16)
            return carry

        def body1(i, carry, q=q, q_cols=q_cols):
            start = pl.multiple_of(256 * i, 256)
            p1[q, pl.ds(start, 256), :] = jnp.dot(
                ncat[pl.ds(768 + start, 256), :], pcat[:, q_cols], preferred_element_type=F32
            ).astype(BF16)
            return carry

        lax.fori_loop(0, 3, body1, 0)
        if s:
            stage1.append(send(p1.at[q], r1.at[s - 1], q1_s.at[s - 1], q1_r.at[s - 1], x_dev(s)))
        lax.fori_loop(0, 3, body0, 0)
        for k in steps:
            to = pl.ds(pl.multiple_of(192 * y_of(k), 64), 192)
            stage0.append(
                send(p0.at[to, q_cols], r0.at[k - 1, :, q_cols], q0_s.at[n, k - 1], q0_r.at[n, k - 1], y_dev(k))
            )
    sends += stage0 + stage1

    def frames_body(i, acc):
        base = pl.multiple_of(32 * i, 32)
        rows = pl.ds(base, 32)
        mean = stat[0, rows, :]
        scale = stat[1, rows, :]
        sum_e = jnp.zeros((32, 128), F32)
        sum_eu = jnp.zeros((32, 128), F32)
        sums = []
        for l in range(12):
            cols = slice(128 * l, 128 * l + 128)
            unit = (packed[rows, cols].astype(F32) - mean) * scale
            up = dn[rows, cols]
            du = up * unit
            sums.append(acc[l] + du[0:8] + du[8:16] + du[16:24] + du[24:32])
            e = up * gain_in[:, cols]
            sum_e = sum_e + e
            sum_eu = sum_eu + e * unit
        e_mean = lane_mean(sum_e)
        eu_mean = lane_mean(sum_eu)
        for l in range(12):
            cols = slice(128 * l, 128 * l + 128)
            unit = (packed[rows, cols].astype(F32) - mean) * scale
            e = dn[rows, cols] * gain_in[:, cols]
            grad_frames[rows, cols] = (
                cext[pl.ds(base + 16, 32), cols].astype(F32) + scale * (e - e_mean - unit * eu_mean)
            ).astype(BF16)
        return tuple(sums)

    in_acc = lax.fori_loop(0, 12, frames_body, tuple(jnp.zeros((8, 128), F32) for _ in range(12)))
    for l in range(12):
        cols = slice(128 * l, 128 * l + 128)
        for j in range(TAPS):
            sa[j : j + 1, cols] = jnp.sum(gk[l, j], axis=0, keepdims=True)
        sa[TAPS : TAPS + 1, cols] = jnp.sum(gain_acc[l], axis=0, keepdims=True)
        sa[32:40, cols] = jnp.broadcast_to(jnp.sum(in_acc[l], axis=0, keepdims=True), (8, 128))

    mine = pl.multiple_of(768 * core, 128)
    other = pl.multiple_of(768 - 768 * core, 128)
    small_a = send(sa.at[:, pl.ds(other, 768)], sb.at[:, 0:768], k_s.at[0], k_r.at[0], sib)

    for copy in stage0:
        copy.wait_recv()
    rows = pl.ds(pl.multiple_of(192 * y, 64), 192)
    for c in range(3):
        cols = slice(512 * c, 512 * c + 512)
        e0[:, cols] = (
            p0[rows, cols].astype(F32) + r0[0, :, cols].astype(F32) + r0[1, :, cols].astype(F32) + r0[2, :, cols].astype(F32)
        ).astype(BF16)
    second0 = [
        send(
            e0.at[:, pl.ds(pl.multiple_of(384 * x_of(s), 128), 384)], s0_in.at[s - 1],
            m0_s.at[s - 1], m0_r.at[s - 1], x_dev(s),
        )
        for s in steps
    ]
    small_a.wait_recv()
    sb[:, 768:1536] = sb[:, 0:768] + sa[:, pl.ds(mine, 768)]
    z_mine = pl.multiple_of(768 + 384 * z_lo, 128)
    z_other = pl.multiple_of(768 + 384 - 384 * z_lo, 128)
    small_b = send(sb.at[:, pl.ds(z_other, 384)], sy.at[4], k_s.at[1], k_r.at[1], pair)
    for copy in stage1:
        copy.wait_recv()
    for c in range(3):
        rows_c = slice(256 * c, 256 * c + 256)
        e1[rows_c, :] = (
            p1[x, rows_c, :].astype(F32) + r1[0, rows_c, :].astype(F32) + r1[1, rows_c, :].astype(F32) + r1[2, rows_c, :].astype(F32)
        ).astype(BF16)
    second1 = [
        send(
            e1.at[pl.ds(pl.multiple_of(192 * y_of(s), 64), 192), :], s1_in.at[s - 1],
            m1_s.at[s - 1], m1_r.at[s - 1], y_dev(s),
        )
        for s in steps
    ]
    small_b.wait_recv()
    sy[pl.ds(y, 1)] = (sb[:, pl.ds(z_mine, 384)] + sy[4])[None]
    y_small = [send(sy.at[y], sy.at[y], ky_s.at[s - 1], ky_r.at[s - 1], y_dev(s)) for s in steps]

    for copy in second0:
        copy.wait_recv()
    x_cols = pl.ds(pl.multiple_of(384 * x, 128), 384)
    sum0 = (
        e0[:, x_cols].astype(F32) + s0_in[0].astype(F32) + s0_in[1].astype(F32) + s0_in[2].astype(F32)
    ).astype(BF16)
    f[0, 0:96, :] = sum0[0:96, :]
    f[1, 0:96, :] = sum0[96:192, :]
    for copy in second1:
        copy.wait_recv()
    sum1 = (
        e1[rows, :].astype(F32) + s1_in[0].astype(F32) + s1_in[1].astype(F32) + s1_in[2].astype(F32)
    ).astype(BF16)
    f[0, 96:192, :] = sum1[0:96, :]
    f[1, 96:192, :] = sum1[96:192, :]
    third = []
    for s in (1, 3, 2, 0):
        for same in (False, True):
            if s or not same:
                n = 2 * s + (0 if same else 1)
                zb = z_lo if same else 1 - z_lo
                third.append(
                    send(
                        f.at[zb, pl.ds(pl.multiple_of(48 * z_of(s), 16), 48), :], u_in.at[n],
                        u_s.at[n], u_r.at[n], z_dev(s, same),
                    )
                )
    for copy in y_small:
        copy.wait_recv()
    sx[pl.ds(x, 1)] = (sy[0] + sy[1] + sy[2] + sy[3])[None]
    x_small = [send(sx.at[x], sx.at[x], kx_s.at[s - 1], kx_r.at[s - 1], x_dev(s)) for s in steps]
    for copy in third:
        copy.wait_recv()

    z_rows = pl.ds(pl.multiple_of(48 * z_hi, 16), 48)
    total = f[z_lo, z_rows, :].astype(F32)
    for n in range(1, 8):
        total = total + u_in[n].astype(F32)
    w_grad[pl.ds(core, 1), z_rows, x_cols] = total.astype(BF16)[None]
    piece = w_grad.at[core, z_rows, x_cols]
    fifth = [send(piece, piece, v_s.at[s - 1], v_r.at[s - 1], z_dev(s, True)) for s in steps]
    for copy in x_small:
        copy.wait_recv()
    sz[pl.ds(z_hi, 1)] = (sx[0] + sx[1] + sx[2] + sx[3])[None]
    z_small = [send(sz.at[z_hi], sz.at[z_hi], kz_s.at[s - 1], kz_r.at[s - 1], z_dev(s, True)) for s in steps]
    for copy in fifth:
        copy.wait_recv()
    strip = w_grad.at[core, :, x_cols]
    sixth = [send(strip, strip, x_s.at[s - 1], x_r.at[s - 1], x_dev(s)) for s in steps]
    seventh = [send(strip, strip, c_s.at[1], c_r.at[1], sib)]
    for copy in z_small:
        copy.wait_recv()
    col_here = pl.multiple_of(768 * core + 384 * z_lo, 128)
    small[:, pl.ds(col_here, 384)] = sz[0] + sz[1] + sz[2] + sz[3]
    here = small.at[:, pl.ds(col_here, 384)]
    small_z = send(here, here, k_s.at[2], k_r.at[2], pair)
    small_here = send(here, here, k_s.at[3], k_r.at[3], sib)
    for n, s in enumerate(steps):
        sixth[n].wait_recv()
        came = w_grad.at[core, :, pl.ds(pl.multiple_of(384 * x_of(4 - s), 128), 384)]
        seventh.append(send(came, came, c_s.at[1 + s], c_r.at[1 + s], sib))
    small_z.wait_recv()
    there = small.at[:, pl.ds(pl.multiple_of(768 * core + 384 - 384 * z_lo, 128), 384)]
    small_there = send(there, there, k_s.at[4], k_r.at[4], sib)
    small_here.wait_recv()
    small_there.wait_recv()
    for copy in seventh:
        copy.wait_recv()
    sends += [small_a, small_b, small_z, small_here, small_there]
    sends += y_small + x_small + z_small + second0 + second1 + third + fifth + sixth + seventh
    for copy in sends + halos + a_copies + y_copies + z_copies + b_copies:
        copy.wait_send()


def block(frames, dest, segment, w, gain, cot, kern, gain_m):
    vm = pl.BlockSpec(memory_space=pltpu.VMEM)
    hbm = pl.BlockSpec(memory_space=pl.ANY)
    sems = pltpu.SemaphoreType.DMA
    three = [sems((3,)), sems((3,))]
    return pl.pallas_call(
        block_kernel,
        out_shape=(
            jax.ShapeDtypeStruct((ROWS, D), BF16),
            jax.ShapeDtypeStruct((ROWS, D), BF16),
            jax.ShapeDtypeStruct((2, 192, D), BF16),
            jax.ShapeDtypeStruct((40, D), F32),
        ),
        in_specs=[vm, vm, vm, hbm, vm, hbm, vm, vm],
        out_specs=(vm, vm, vm, vm),
        scratch_shapes=[
            pltpu.VMEM((ROWS, D), BF16),
            pltpu.VMEM((ROWS, D), F32),
            pltpu.VMEM((ROWS, D), F32),
            pltpu.VMEM((448, D), BF16),
            pltpu.VMEM((416, D), BF16),
            pltpu.VMEM((448, 128), jnp.int32),
            pltpu.VMEM((2, ROWS, 128), F32),
            pltpu.VMEM((D, 2 * D), BF16),
            pltpu.VMEM((ROWS, D + 128), BF16),
            pltpu.VMEM((ROWS, D + 128), BF16),
            pltpu.VMEM((ROWS, D), BF16),
            pltpu.VMEM((12, 448, 128), F32),
            pltpu.VMEM((12, 416, 128), F32),
            pltpu.VMEM((12, 416, 128), F32),
            pltpu.VMEM((12, TAPS, 8, 128), F32),
            pltpu.VMEM((12, TAPS, 8, 128), F32),
            pltpu.VMEM((448, 128), jnp.int32),
            pltpu.VMEM((416, 128), F32),
            pltpu.VMEM((2, 416, 128), F32),
            pltpu.VMEM((D, 768), BF16),
            pltpu.VMEM((768, D), BF16),
            pltpu.VMEM((ROWS, D), BF16),
            pltpu.VMEM((ROWS, D), F32),
            pltpu.VMEM((768, D), BF16),
            pltpu.VMEM((4, 768, 384), BF16),
            pltpu.VMEM((3, 192, D), BF16),
            pltpu.VMEM((3, 768, 384), BF16),
            pltpu.VMEM((192, D), BF16),
            pltpu.VMEM((768, 384), BF16),
            pltpu.VMEM((3, 192, 384), BF16),
            pltpu.VMEM((3, 192, 384), BF16),
            pltpu.VMEM((2, 192, 384), BF16),
            pltpu.VMEM((8, 48, 384), BF16),
            pltpu.VMEM((40, D), F32),
            pltpu.VMEM((40, D), F32),
            pltpu.VMEM((5, 40, 384), F32),
            pltpu.VMEM((4, 40, 384), F32),
            pltpu.VMEM((4, 40, 384), F32),
            sems((7,)), sems((7,)),
            *three,
            sems((2, 4)), sems((2, 4)),
            sems((7,)), sems((7,)),
            sems((6,)), sems((6,)),
            sems((4,)),
            sems((5,)), sems((5,)),
            sems((4, 3)), sems((4, 3)),
            *three, *three, *three,
            sems((8,)), sems((8,)),
            *three, *three,
            sems((4,)), sems((4,)),
            sems((5,)), sems((5,)),
            *three, *three, *three,
        ],
        compiler_params=pltpu.CompilerParams(
            collective_id=0, has_side_effects=True, vmem_limit_bytes=VMEM_LIMIT
        ),
        name="block",
    )(frames, dest, segment, w, gain, cot, kern, gain_m)


def tail_kernel(w_grad, small, grad_weight, g_in, g_kernel, g_mid):
    for c in range(2):
        grad_weight[:, D * c : D * c + D] = w_grad[c].astype(F32)
    g_in[...] = small[32:33, :].reshape(D)
    g_kernel[...] = small[:TAPS, :]
    g_mid[...] = small[TAPS : TAPS + 1, :].reshape(D)


def tail(w_grad, small):
    vm = pl.BlockSpec(memory_space=pltpu.VMEM)
    return pl.pallas_call(
        tail_kernel,
        out_shape=(
            jax.ShapeDtypeStruct((192, 2 * D), F32),
            jax.ShapeDtypeStruct((D,), F32),
            jax.ShapeDtypeStruct((TAPS, D), F32),
            jax.ShapeDtypeStruct((D,), F32),
        ),
        in_specs=[vm] * 2,
        out_specs=(vm,) * 4,
        name="tail",
    )(w_grad, small)


def on_device(frames_in, dest, segment, gain_in, w_glu, kernel, gain_mid, cotangent):
    output, grad_frames, w_grad, small = block(
        frames_in, dest, segment, w_glu, gain_in, cotangent, kernel, gain_mid
    )
    return (output, grad_frames, *tail(w_grad, small))


def solution(mesh):
    return jax.shard_map(
        on_device,
        mesh=mesh,
        in_specs=(
            P(("dp", "fsdp"), None),
            P(("dp", "fsdp")),
            P("dp", "fsdp"),
            P(),
            P("fsdp", None),
            P(),
            P(),
            P(("dp", "fsdp"), None),
        ),
        out_specs=(
            P(("dp", "fsdp"), None),
            P(("dp", "fsdp"), None),
            P("fsdp", None),
            P(),
            P(),
            P(),
        ),
        check_vma=False,
    )
```

```python
import jax
import jax.numpy as jnp
from jax import lax
from jax.experimental import pallas as pl
from jax.experimental.pallas import tpu as pltpu
from jax.sharding import PartitionSpec as P

EPS = 1e-05
ROWS = 384
D = 1536
TAPS = 31
MESH = pl.DeviceIdType.MESH
F32 = jnp.float32
BF16 = jnp.bfloat16
VMEM_LIMIT = 61 * 1024 * 1024


def place():
    dp = lax.axis_index("dp")
    me = lax.axis_index("fsdp")
    z_hi = lax.div(dp, 8)
    x = lax.rem(lax.div(dp, 2), 4)
    core = lax.rem(dp, 2)
    return dp, me, z_hi, x, core, lax.div(me, 2), lax.rem(me, 2)


def send(src, dst, send_sem, recv_sem, target):
    copy = pltpu.make_async_remote_copy(
        src_ref=src, dst_ref=dst, send_sem=send_sem, recv_sem=recv_sem, device_id=target, device_id_type=MESH
    )
    copy.start()
    return copy


def greet(targets):
    barrier = pltpu.get_barrier_semaphore()
    for target in targets:
        pl.semaphore_signal(barrier, inc=1, device_id=target, device_id_type=MESH)
    pl.semaphore_wait(barrier, len(targets))


def sigmoid(v):
    return 0.5 * jnp.tanh(0.5 * v) + 0.5


def vec_mean(v):
    return jnp.sum(v, axis=-1, keepdims=True) * (1.0 / D)


def block_kernel(
    frames, dest, segment, w, gain, cot, kern, gain_m,
    output, grad_frames, w_grad, small,
    packed, value, sig, gext, cext, sext, stat,
    w_all, out_buf, in_buf, normed, normed_k, gx, mx, ex, kb, gk, seg, s1, s2,
    ncat, pcat, psend, dn, p0, p1, r0, r1, e0, e1, s0_in, s1_in, f, u_in, sa, sb, sy, sx, sz,
    a_s, a_r, y_s, y_r, z_s, z_r, w_s, w_r, b_s, b_r, h_s, h_r, l_s,
    c_s, c_r, q0_s, q0_r, q1_s, q1_r, m0_s, m0_r, m1_s, m1_r, u_s, u_r, v_s, v_r, x_s, x_r, d_s, d_r,
    k_s, k_r, ky_s, ky_r, kx_s, kx_r, kz_s, kz_r,
):
    dp, me, z_hi, x, core, y, z_lo = place()
    sib = (dp + 1 - 2 * core, me)
    up = (lax.rem(z_hi + z_lo, 4) * 8 + x * 2 + core, me + 1 - 2 * z_lo)
    down = (lax.rem(z_hi + 3 + z_lo, 4) * 8 + x * 2 + core, me + 1 - 2 * z_lo)
    far = (lax.rem(z_hi + 3 + 2 * z_lo, 4) * 8 + x * 2 + core, me + 1 - 2 * z_lo)
    nxt = (dp, lax.rem(me + 1, 8))
    prv = (dp, lax.rem(me + 7, 8))

    steps = (1, 3, 2)

    def x_of(s):
        return lax.rem(x + s, 4)

    def y_of(s):
        return lax.rem(y + s, 4)

    def z_of(s):
        return lax.rem(z_hi + s, 4)

    def x_dev(s):
        return (z_hi * 8 + x_of(s) * 2 + core, me)

    def y_dev(s):
        return (dp, 2 * y_of(s) + z_lo)

    def z_dev(s, same):
        return (z_of(s) * 8 + x * 2 + core, me if same else me + 1 - 2 * z_lo)

    pair = (dp, me + 1 - 2 * z_lo)
    greet(
        [(dp, lax.rem(me + s, 8)) for s in range(1, 8)]
        + [sib]
        + [x_dev(s) for s in steps]
        + [z_dev(s, True) for s in steps]
        + [z_dev(s, False) for s in steps]
    )
    sends = []

    half = core * 96
    par = lax.rem(x, 2)
    c_mine = pl.multiple_of(D * par, 128)
    c_else = pl.multiple_of(D - D * par, 128)
    c_low = pl.ds(c_mine, 768)
    c_high = pl.ds(pl.multiple_of(c_mine + 768, 128), 768)

    def rows_of(shard):
        return pl.ds(pl.multiple_of(192 * shard + half, 32), 96)

    own_rows = pl.ds(pl.multiple_of(half, 32), 96)
    y_copies = []
    for s in steps:
        y_copies.append(
            send(
                w.at[own_rows, pl.ds(c_mine, D)], w_all.at[rows_of(me), pl.ds(c_mine, D)],
                y_s.at[s - 1], y_r.at[s - 1], y_dev(s),
            )
        )
    z_copies = [
        send(w.at[own_rows, c_high], w_all.at[rows_of(me), c_high], z_s.at[0, 0], z_r.at[0, 0], up),
        send(w.at[own_rows, c_low], w_all.at[rows_of(me), c_low], z_s.at[1, 0], z_r.at[1, 0], down),
    ]
    sext[32:416, :] = jnp.broadcast_to(segment[...].astype(F32), (128, ROWS)).T.astype(jnp.int32)
    halos = [
        send(cot.at[368:384, :], cext.at[0:16, :], h_s.at[0], h_r.at[0], nxt),
        send(cot.at[0:16, :], cext.at[400:416, :], h_s.at[1], h_r.at[1], prv),
        send(sext.at[384:416, :], sext.at[0:32, :], h_s.at[2], h_r.at[2], nxt),
        send(sext.at[32:64, :], sext.at[416:448, :], h_s.at[3], h_r.at[3], prv),
    ]
    cot_copy = pltpu.make_async_copy(cot, cext.at[16:400, :], l_s.at[0])
    cot_copy.start()

    d = dest[...].reshape(1, ROWS)
    gain_in = gain[...].reshape(1, D)
    k8 = lax.broadcasted_iota(jnp.int32, (8, ROWS), 0)
    rel = d - ROWS * k8
    hot = jnp.logical_and(rel >= 0, rel < ROWS)
    hot_f = jnp.where(hot, 1.0, 0.0).astype(F32)
    before = lax.broadcasted_iota(jnp.int32, (ROWS, ROWS), 0) < lax.broadcasted_iota(jnp.int32, (ROWS, ROWS), 1)
    rank = jnp.dot(hot_f.astype(BF16), jnp.where(before, 1.0, 0.0).astype(BF16), preferred_element_type=F32)
    order = jnp.sum(hot_f * (rank + 48.0 * k8.astype(F32)), axis=0, keepdims=True)
    slot = jnp.sum(hot_f * rel.astype(F32), axis=0, keepdims=True)
    high = jnp.floor(slot * (1.0 / 16.0))
    low = slot - 16.0 * high
    row_id = lax.broadcasted_iota(jnp.int32, (ROWS, ROWS), 0).astype(F32)
    perm = jnp.where(row_id == order, 1.0, 0.0).astype(BF16)
    tag_row = lax.broadcasted_iota(jnp.int32, (128, ROWS), 0)
    tags = jnp.where(tag_row == 0, high, jnp.where(tag_row == 1, low, 0.0)).astype(BF16)
    out_buf[:, D:] = lax.dot_general(perm, tags, (((1,), (1,)), ((), ())), preferred_element_type=F32).astype(BF16)
    for c in range(3):
        out_buf[:, 512 * c : 512 * c + 512] = jnp.dot(
            perm, frames[:, 512 * c : 512 * c + 512], preferred_element_type=F32
        ).astype(BF16)
    a_copies = []
    for s in (1, 7, 2, 6, 3, 5, 4):
        peer = lax.rem(me + s, 8)
        a_copies.append(
            send(
                out_buf.at[pl.ds(48 * peer, 48), :], in_buf.at[pl.ds(48 * me, 48), :],
                a_s.at[s - 1], a_r.at[s - 1], (dp, peer),
            )
        )
    own = pltpu.make_async_copy(out_buf.at[pl.ds(48 * me, 48), :], in_buf.at[pl.ds(48 * me, 48), :], l_s.at[1])
    own.start()
    own_w = pltpu.make_async_copy(w, w_all.at[pl.ds(192 * me, 192), :], l_s.at[2])
    own_w.start()

    b_copies, w_copies = {}, {}
    shards = [2 * lax.rem(y + 4 - s, 4) + z_lo for s in steps]
    shards += [2 * lax.rem(y + 4 - t, 4) + 1 - z_lo for t in (0,) + steps]

    def pass_on(shard, index):
        rows = rows_of(shard)
        high, low_piece = w_all.at[rows, c_high], w_all.at[rows, c_low]
        w_copies[index] = [
            send(high, high, w_s.at[0, index], w_r.at[0, index], x_dev(1)),
            send(low_piece, low_piece, w_s.at[1, index], w_r.at[1, index], x_dev(3)),
        ]
        piece = w_all.at[rows, pl.ds(c_mine, D)]
        b_copies[0, index] = send(piece, piece, b_s.at[0, index], b_r.at[0, index], sib)

    def y_arrived(n, s):
        y_copies[n].wait_recv()
        shard = shards[n]
        rows = rows_of(shard)
        high, low_piece = w_all.at[rows, c_high], w_all.at[rows, c_low]
        z_copies.append(send(high, high, z_s.at[0, s], z_r.at[0, s], up))
        z_copies.append(send(low_piece, low_piece, z_s.at[1, s], z_r.at[1, s], down))
        pass_on(shard, n)

    def z_arrived(n):
        z_copies[2 * n].wait_recv()
        z_copies[2 * n + 1].wait_recv()
        pass_on(shards[3 + n], 3 + n)

    def x_arrived(index):
        for copy in w_copies[index]:
            copy.wait_recv()
        shard = shards[index]
        piece = w_all.at[rows_of(shard), pl.ds(c_else, D)]
        b_copies[1, index] = send(piece, piece, b_s.at[1, index], b_r.at[1, index], sib)

    y_arrived(0, 1)
    y_arrived(1, 3)
    z_arrived(0)
    y_arrived(2, 2)

    own.wait()
    for copy in a_copies:
        copy.wait_recv()
    tag = in_buf[:, D:].astype(F32)
    at = tag[:, 0:1] * 16.0 + tag[:, 1:2]
    col_id = lax.broadcasted_iota(jnp.int32, (ROWS, ROWS), 1).astype(F32)
    unperm = jnp.where(col_id == at, 1.0, 0.0).T.astype(BF16)
    for c in range(3):
        packed[:, 512 * c : 512 * c + 512] = jnp.dot(
            unperm, in_buf[:, 512 * c : 512 * c + 512], preferred_element_type=F32
        ).astype(BF16)

    z_arrived(1)
    z_arrived(2)

    def norm_body(i, carry):
        rows = pl.ds(pl.multiple_of(32 * i, 32), 32)
        v = packed[rows, :].astype(F32)
        mean = vec_mean(v)
        centre = v - mean
        scale = lax.rsqrt(vec_mean(centre * centre) + EPS)
        stat[0, rows, :] = jnp.broadcast_to(mean, (32, 128))
        stat[1, rows, :] = jnp.broadcast_to(scale, (32, 128))
        unit = (centre * scale * gain_in).astype(BF16)
        normed[rows, :] = unit
        for c in range(4):
            for z in range(2):
                at = 384 * c + 192 * z
                normed_k[z, c, rows, :] = unit[:, at : at + 192]
        return carry

    lax.fori_loop(0, 12, norm_body, 0)
    z_arrived(3)
    for index in (0, 1, 3, 2):
        x_arrived(index)
    for c in range(4):
        flipped = normed[:, 384 * c : 384 * c + 384].astype(F32).T.astype(BF16)
        for z in range(2):
            for p in range(2):
                to = 768 * p + 192 * c + 96 * z
                ncat[to : to + 96, 0:384] = flipped[192 * z + 96 * p : 192 * z + 96 * p + 96, :]
    share = send(ncat.at[:, 0:384], ncat.at[:, 384:768], c_s.at[0], c_r.at[0], sib)
    sends.append(share)
    for index in (4, 5, 6):
        x_arrived(index)

    def proj(z, cols):
        total = None
        for c in range(4):
            rows = pl.ds(pl.multiple_of(384 * c + 192 * z, 64), 192)
            part = jnp.dot(normed_k[z, c], w_all[rows, cols], preferred_element_type=F32)
            total = part if total is None else total + part
        return total

    def proj_body(i, carry):
        left = pl.ds(pl.multiple_of(256 * i, 256), 256)
        right = pl.ds(pl.multiple_of(256 * i + D, 256), 256)
        value[:, left] = proj(z_lo, left)
        sig[:, left] = proj(z_lo, right)
        return carry

    def proj_rest(i, carry):
        left = pl.ds(pl.multiple_of(256 * i, 256), 256)
        right = pl.ds(pl.multiple_of(256 * i + D, 256), 256)
        v = value[:, left] + proj(1 - z_lo, left)
        s = sigmoid(sig[:, left] + proj(1 - z_lo, right))
        value[:, left] = v
        sig[:, left] = s
        gext[32:416, left] = (v * s).astype(BF16)
        return carry

    own_w.wait()
    for index in (0, 1, 2):
        b_copies[0, index].wait_recv()
        b_copies[1, index].wait_recv()
    lax.fori_loop(0, 6, proj_body, 0)
    for index in (3, 4, 5, 6):
        b_copies[0, index].wait_recv()
        b_copies[1, index].wait_recv()
    lax.fori_loop(0, 6, proj_rest, 0)
    halos.append(send(gext.at[384:416, :], gext.at[0:32, :], h_s.at[4], h_r.at[4], nxt))
    halos.append(send(gext.at[32:64, :], gext.at[416:448, :], h_s.at[5], h_r.at[5], prv))

    for l in range(12):
        cols = slice(128 * l, 128 * l + 128)
        gx[l, 32:416, :] = gext[32:416, cols].astype(F32)
        for j in range(TAPS):
            kb[l, j] = jnp.broadcast_to(kern[j : j + 1, cols], (8, 128))
    gk[...] = jnp.zeros_like(gk)
    s1[...] = jnp.zeros_like(s1)
    cot_copy.wait()
    for copy in halos:
        copy.wait_recv()
    for l in range(12):
        cols = slice(128 * l, 128 * l + 128)
        gx[l, 0:32, :] = gext[0:32, cols].astype(F32)
        gx[l, 416:448, :] = gext[416:448, cols].astype(F32)
    edge = lax.broadcasted_iota(jnp.int32, (448, 128), 0) + ROWS * me - 32
    seg[...] = jnp.where(jnp.logical_and(edge >= 0, edge < 8 * ROWS), sext[...], -1)

    def conv_block(n, carry):
        base = pl.multiple_of(32 * lax.div(n, 4), 32)
        l0 = 3 * lax.rem(n, 4)
        total = [[jnp.zeros((8, 128), F32) for _ in range(4)] for _ in range(3)]
        here = [seg[pl.ds(base + 16 + 8 * t, 8), :] for t in range(4)]
        for j in range(TAPS):
            taps = [kb[l0 + i, j] for i in range(3)]
            for t in range(4):
                at = pl.ds(base + 1 + j + 8 * t, 8)
                same = seg[at, :] == here[t]
                for i in range(3):
                    total[i][t] = total[i][t] + jnp.where(same, gx[l0 + i, at, :], 0.0) * taps[i]
        for t in range(4):
            at = pl.ds(base + 8 * t, 8)
            for i in range(3):
                mx[l0 + i, at, :] = total[i][t]
            s1[at, :] += total[0][t] + total[1][t] + total[2][t]
        return carry

    lax.fori_loop(0, 52, conv_block, 0)

    def lane_mean(v):
        return jnp.broadcast_to(jnp.sum(v, axis=-1, keepdims=True) * (1.0 / D), v.shape)

    def stat_block(i, carry):
        rows = pl.ds(pl.multiple_of(104 * i, 8), 104)
        mean = lane_mean(s1[rows, :])
        square = jnp.zeros((104, 128), F32)
        for l in range(12):
            centre = mx[l, rows, :] - mean
            mx[l, rows, :] = centre
            square = square + centre * centre
        s1[rows, :] = lax.rsqrt(lane_mean(square) + EPS)
        return carry

    lax.fori_loop(0, 4, stat_block, 0)
    gain_mid = gain_m[...].reshape(1, D)

    def gate_rows(base, size, own, acc):
        rows = pl.ds(base, size)
        scale = s1[rows, :]
        sum_e = jnp.zeros((size, 128), F32)
        sum_eu = jnp.zeros((size, 128), F32)
        sums = []
        for l in range(12):
            cols = slice(128 * l, 128 * l + 128)
            unit = mx[l, rows, :] * scale
            mid = unit * gain_mid[:, cols]
            s = sigmoid(mid)
            gated = mid * s
            d_mid = cext[rows, cols].astype(F32) * (s + gated * (1.0 - s))
            if own:
                to = pl.ds(base - 16, size)
                output[to, cols] = (packed[to, cols].astype(F32) + gated).astype(BF16)
                du = d_mid * unit
                part = acc[l]
                for t in range(size // 8):
                    part = part + du[8 * t : 8 * t + 8, :]
                sums.append(part)
            e = d_mid * gain_mid[:, cols]
            sum_e = sum_e + e
            sum_eu = sum_eu + e * unit
            mx[l, rows, :] = unit
            ex[l, rows, :] = e
        s2[0, rows, :] = sum_e
        s2[1, rows, :] = sum_eu
        return tuple(sums)

    gate_rows(0, 16, False, None)
    gate_rows(400, 16, False, None)
    gain_acc = lax.fori_loop(
        0, 12, lambda i, acc: gate_rows(pl.multiple_of(16 + 32 * i, 16), 32, True, acc),
        tuple(jnp.zeros((8, 128), F32) for _ in range(12)),
    )

    def mixed_block(i, carry):
        rows = pl.ds(pl.multiple_of(104 * i, 8), 104)
        e_mean = lane_mean(s2[0, rows, :])
        eu_mean = lane_mean(s2[1, rows, :])
        scale = s1[rows, :]
        for l in range(12):
            mx[l, rows, :] = scale * (ex[l, rows, :] - e_mean - mx[l, rows, :] * eu_mean)
        return carry

    lax.fori_loop(0, 4, mixed_block, 0)

    stage0, stage1 = [], []
    own_half = pl.multiple_of(D * core, 128)
    other_half = pl.multiple_of(D - D * core, 128)
    for n, s in enumerate((1, 3, 2, 0)):
        q = x_of(s)
        q0 = pl.multiple_of(384 * q, 128)
        q_cols = pl.ds(q0, 384)
        l0 = 3 * q

        def back_block(b, carry, l0=l0, q0=q0):
            base = pl.multiple_of(32 * b, 32)
            total = [[jnp.zeros((8, 128), F32) for _ in range(4)] for _ in range(3)]
            glu = [[gx[l0 + i, pl.ds(base + 32 + 8 * t, 8), :] for t in range(4)] for i in range(3)]
            here = [seg[pl.ds(base + 32 + 8 * t, 8), :] for t in range(4)]
            for j in range(TAPS):
                taps = [kb[l0 + i, TAPS - 1 - j] for i in range(3)]
                grads = [None] * 3
                for t in range(4):
                    same = seg[pl.ds(base + 17 + j + 8 * t, 8), :] == here[t]
                    at = pl.ds(base + 1 + j + 8 * t, 8)
                    for i in range(3):
                        v = jnp.where(same, mx[l0 + i, at, :], 0.0)
                        total[i][t] = total[i][t] + v * taps[i]
                        grads[i] = glu[i][t] * v if t == 0 else grads[i] + glu[i][t] * v
                for i in range(3):
                    gk[l0 + i, TAPS - 1 - j] += grads[i]
            for i in range(3):
                cols = pl.ds(pl.multiple_of(q0 + 128 * i, 128), 128)
                for t in range(2):
                    rows = pl.ds(base + 16 * t, 16)
                    d_glu = jnp.concatenate([total[i][2 * t], total[i][2 * t + 1]], axis=0)
                    sg = sig[rows, cols]
                    d_value = d_glu * sg
                    d_gate = d_value * value[rows, cols] * (1.0 - sg)
                    pcat[rows, cols] = jnp.where(core == 0, d_value, d_gate).astype(BF16)
                    psend[rows, cols] = jnp.where(core == 0, d_gate, d_value).astype(BF16)
            return carry

        lax.fori_loop(0, 12, back_block, 0)
        swap = send(psend.at[:, q_cols], pcat.at[384:768, q_cols], d_s.at[n], d_r.at[n], sib)
        sends.append(swap)
        own_cols = pl.ds(pl.multiple_of(own_half + q0, 128), 384)
        other_cols = pl.ds(pl.multiple_of(other_half + q0, 128), 384)

        def dn_body(i, carry, n=n, q_cols=q_cols, own_cols=own_cols, other_cols=other_cols):
            cols = pl.ds(pl.multiple_of(256 * i, 256), 256)
            dims = (((1,), (1,)), ((), ()))
            part = lax.dot_general(
                pcat[0:384, q_cols], w_all[cols, own_cols], dims, preferred_element_type=F32
            ) + lax.dot_general(psend[:, q_cols], w_all[cols, other_cols], dims, preferred_element_type=F32)
            dn[:, cols] = part if n == 0 else dn[:, cols] + part
            return carry

        lax.fori_loop(0, 6, dn_body, 0)
        if n == 0:
            share.wait_recv()
        swap.wait_recv()

        def body0(i, carry, q_cols=q_cols):
            rows = pl.ds(pl.multiple_of(256 * i, 256), 256)
            p0[rows, q_cols] = jnp.dot(ncat[rows, :], pcat[:, q_cols], preferred_element_type=F32).astype(BF16)
            return carry

        def body1(i, carry, q=q, q_cols=q_cols):
            start = pl.multiple_of(256 * i, 256)
            p1[q, pl.ds(start, 256), :] = jnp.dot(
                ncat[pl.ds(768 + start, 256), :], pcat[:, q_cols], preferred_element_type=F32
            ).astype(BF16)
            return carry

        lax.fori_loop(0, 3, body1, 0)
        if s:
            stage1.append(send(p1.at[q], r1.at[s - 1], q1_s.at[s - 1], q1_r.at[s - 1], x_dev(s)))
        lax.fori_loop(0, 3, body0, 0)
        for k in steps:
            to = pl.ds(pl.multiple_of(192 * y_of(k), 64), 192)
            stage0.append(
                send(p0.at[to, q_cols], r0.at[k - 1, :, q_cols], q0_s.at[n, k - 1], q0_r.at[n, k - 1], y_dev(k))
            )
    sends += stage0 + stage1

    def frames_body(i, acc):
        base = pl.multiple_of(32 * i, 32)
        rows = pl.ds(base, 32)
        mean = stat[0, rows, :]
        scale = stat[1, rows, :]
        sum_e = jnp.zeros((32, 128), F32)
        sum_eu = jnp.zeros((32, 128), F32)
        sums = []
        for l in range(12):
            cols = slice(128 * l, 128 * l + 128)
            unit = (packed[rows, cols].astype(F32) - mean) * scale
            up = dn[rows, cols]
            du = up * unit
            sums.append(acc[l] + du[0:8] + du[8:16] + du[16:24] + du[24:32])
            e = up * gain_in[:, cols]
            sum_e = sum_e + e
            sum_eu = sum_eu + e * unit
        e_mean = lane_mean(sum_e)
        eu_mean = lane_mean(sum_eu)
        for l in range(12):
            cols = slice(128 * l, 128 * l + 128)
            unit = (packed[rows, cols].astype(F32) - mean) * scale
            e = dn[rows, cols] * gain_in[:, cols]
            grad_frames[rows, cols] = (
                cext[pl.ds(base + 16, 32), cols].astype(F32) + scale * (e - e_mean - unit * eu_mean)
            ).astype(BF16)
        return tuple(sums)

    in_acc = lax.fori_loop(0, 12, frames_body, tuple(jnp.zeros((8, 128), F32) for _ in range(12)))
    for l in range(12):
        cols = slice(128 * l, 128 * l + 128)
        for j in range(TAPS):
            sa[j : j + 1, cols] = jnp.sum(gk[l, j], axis=0, keepdims=True)
        sa[TAPS : TAPS + 1, cols] = jnp.sum(gain_acc[l], axis=0, keepdims=True)
        sa[32:40, cols] = jnp.broadcast_to(jnp.sum(in_acc[l], axis=0, keepdims=True), (8, 128))

    mine = pl.multiple_of(768 * core, 128)
    other = pl.multiple_of(768 - 768 * core, 128)
    small_a = send(sa.at[:, pl.ds(other, 768)], sb.at[:, 0:768], k_s.at[0], k_r.at[0], sib)

    for copy in stage0:
        copy.wait_recv()
    rows = pl.ds(pl.multiple_of(192 * y, 64), 192)
    for c in range(3):
        cols = slice(512 * c, 512 * c + 512)
        e0[:, cols] = (
            p0[rows, cols].astype(F32) + r0[0, :, cols].astype(F32) + r0[1, :, cols].astype(F32) + r0[2, :, cols].astype(F32)
        ).astype(BF16)
    second0 = [
        send(
            e0.at[:, pl.ds(pl.multiple_of(384 * x_of(s), 128), 384)], s0_in.at[s - 1],
            m0_s.at[s - 1], m0_r.at[s - 1], x_dev(s),
        )
        for s in steps
    ]
    small_a.wait_recv()
    sb[:, 768:1536] = sb[:, 0:768] + sa[:, pl.ds(mine, 768)]
    z_mine = pl.multiple_of(768 + 384 * z_lo, 128)
    z_other = pl.multiple_of(768 + 384 - 384 * z_lo, 128)
    small_b = send(sb.at[:, pl.ds(z_other, 384)], sy.at[4], k_s.at[1], k_r.at[1], pair)
    for copy in stage1:
        copy.wait_recv()
    for c in range(3):
        rows_c = slice(256 * c, 256 * c + 256)
        e1[rows_c, :] = (
            p1[x, rows_c, :].astype(F32) + r1[0, rows_c, :].astype(F32) + r1[1, rows_c, :].astype(F32) + r1[2, rows_c, :].astype(F32)
        ).astype(BF16)
    second1 = [
        send(
            e1.at[pl.ds(pl.multiple_of(192 * y_of(s), 64), 192), :], s1_in.at[s - 1],
            m1_s.at[s - 1], m1_r.at[s - 1], y_dev(s),
        )
        for s in steps
    ]
    small_b.wait_recv()
    sy[pl.ds(y, 1)] = (sb[:, pl.ds(z_mine, 384)] + sy[4])[None]
    y_small = [send(sy.at[y], sy.at[y], ky_s.at[s - 1], ky_r.at[s - 1], y_dev(s)) for s in steps]

    for copy in second0:
        copy.wait_recv()
    x_cols = pl.ds(pl.multiple_of(384 * x, 128), 384)
    sum0 = (
        e0[:, x_cols].astype(F32) + s0_in[0].astype(F32) + s0_in[1].astype(F32) + s0_in[2].astype(F32)
    ).astype(BF16)
    f[0, 0:96, :] = sum0[0:96, :]
    f[1, 0:96, :] = sum0[96:192, :]
    for copy in second1:
        copy.wait_recv()
    sum1 = (
        e1[rows, :].astype(F32) + s1_in[0].astype(F32) + s1_in[1].astype(F32) + s1_in[2].astype(F32)
    ).astype(BF16)
    f[0, 96:192, :] = sum1[0:96, :]
    f[1, 96:192, :] = sum1[96:192, :]
    third = []
    for s in (1, 3, 2, 0):
        for same in (False, True):
            if s or not same:
                n = 2 * s + (0 if same else 1)
                zb = z_lo if same else 1 - z_lo
                third.append(
                    send(
                        f.at[zb, pl.ds(pl.multiple_of(48 * z_of(s), 16), 48), :], u_in.at[n],
                        u_s.at[n], u_r.at[n], z_dev(s, same),
                    )
                )
    for copy in y_small:
        copy.wait_recv()
    sx[pl.ds(x, 1)] = (sy[0] + sy[1] + sy[2] + sy[3])[None]
    x_small = [send(sx.at[x], sx.at[x], kx_s.at[s - 1], kx_r.at[s - 1], x_dev(s)) for s in steps]
    for copy in third:
        copy.wait_recv()

    z_rows = pl.ds(pl.multiple_of(48 * z_hi, 16), 48)
    total = f[z_lo, z_rows, :].astype(F32)
    for n in range(1, 8):
        total = total + u_in[n].astype(F32)
    w_grad[pl.ds(core, 1), z_rows, x_cols] = total.astype(BF16)[None]
    piece = w_grad.at[core, z_rows, x_cols]
    fifth = [send(piece, piece, v_s.at[s - 1], v_r.at[s - 1], z_dev(s, True)) for s in steps]
    for copy in x_small:
        copy.wait_recv()
    sz[pl.ds(z_hi, 1)] = (sx[0] + sx[1] + sx[2] + sx[3])[None]
    z_small = [send(sz.at[z_hi], sz.at[z_hi], kz_s.at[s - 1], kz_r.at[s - 1], z_dev(s, True)) for s in steps]
    for copy in fifth:
        copy.wait_recv()
    strip = w_grad.at[core, :, x_cols]
    sixth = [send(strip, strip, x_s.at[s - 1], x_r.at[s - 1], x_dev(s)) for s in steps]
    seventh = [send(strip, strip, c_s.at[1], c_r.at[1], sib)]
    for copy in z_small:
        copy.wait_recv()
    col_here = pl.multiple_of(768 * core + 384 * z_lo, 128)
    small[:, pl.ds(col_here, 384)] = sz[0] + sz[1] + sz[2] + sz[3]
    here = small.at[:, pl.ds(col_here, 384)]
    small_z = send(here, here, k_s.at[2], k_r.at[2], pair)
    small_here = send(here, here, k_s.at[3], k_r.at[3], sib)
    for n, s in enumerate(steps):
        sixth[n].wait_recv()
        came = w_grad.at[core, :, pl.ds(pl.multiple_of(384 * x_of(4 - s), 128), 384)]
        seventh.append(send(came, came, c_s.at[1 + s], c_r.at[1 + s], sib))
    small_z.wait_recv()
    there = small.at[:, pl.ds(pl.multiple_of(768 * core + 384 - 384 * z_lo, 128), 384)]
    small_there = send(there, there, k_s.at[4], k_r.at[4], sib)
    small_here.wait_recv()
    small_there.wait_recv()
    for copy in seventh:
        copy.wait_recv()
    sends += [small_a, small_b, small_z, small_here, small_there]
    sends += y_small + x_small + z_small + second0 + second1 + third + fifth + sixth + seventh
    for pair_of in w_copies.values():
        sends += pair_of
    for copy in sends + halos + a_copies + y_copies + z_copies + list(b_copies.values()):
        copy.wait_send()


def block(frames, dest, segment, w, gain, cot, kern, gain_m):
    vm = pl.BlockSpec(memory_space=pltpu.VMEM)
    hbm = pl.BlockSpec(memory_space=pl.ANY)
    sems = pltpu.SemaphoreType.DMA
    three = [sems((3,)), sems((3,))]
    return pl.pallas_call(
        block_kernel,
        out_shape=(
            jax.ShapeDtypeStruct((ROWS, D), BF16),
            jax.ShapeDtypeStruct((ROWS, D), BF16),
            jax.ShapeDtypeStruct((2, 192, D), BF16),
            jax.ShapeDtypeStruct((40, D), F32),
        ),
        in_specs=[vm, vm, vm, hbm, vm, hbm, vm, vm],
        out_specs=(vm, vm, vm, vm),
        scratch_shapes=[
            pltpu.VMEM((ROWS, D), BF16),
            pltpu.VMEM((ROWS, D), F32),
            pltpu.VMEM((ROWS, D), F32),
            pltpu.VMEM((448, D), BF16),
            pltpu.VMEM((416, D), BF16),
            pltpu.VMEM((448, 128), jnp.int32),
            pltpu.VMEM((2, ROWS, 128), F32),
            pltpu.VMEM((D, 2 * D), BF16),
            pltpu.VMEM((ROWS, D + 128), BF16),
            pltpu.VMEM((ROWS, D + 128), BF16),
            pltpu.VMEM((ROWS, D), BF16),
            pltpu.VMEM((2, 4, ROWS, 192), BF16),
            pltpu.VMEM((12, 448, 128), F32),
            pltpu.VMEM((12, 416, 128), F32),
            pltpu.VMEM((12, 416, 128), F32),
            pltpu.VMEM((12, TAPS, 8, 128), F32),
            pltpu.VMEM((12, TAPS, 8, 128), F32),
            pltpu.VMEM((448, 128), jnp.int32),
            pltpu.VMEM((416, 128), F32),
            pltpu.VMEM((2, 416, 128), F32),
            pltpu.VMEM((D, 768), BF16),
            pltpu.VMEM((768, D), BF16),
            pltpu.VMEM((ROWS, D), BF16),
            pltpu.VMEM((ROWS, D), F32),
            pltpu.VMEM((768, D), BF16),
            pltpu.VMEM((4, 768, 384), BF16),
            pltpu.VMEM((3, 192, D), BF16),
            pltpu.VMEM((3, 768, 384), BF16),
            pltpu.VMEM((192, D), BF16),
            pltpu.VMEM((768, 384), BF16),
            pltpu.VMEM((3, 192, 384), BF16),
            pltpu.VMEM((3, 192, 384), BF16),
            pltpu.VMEM((2, 192, 384), BF16),
            pltpu.VMEM((8, 48, 384), BF16),
            pltpu.VMEM((40, D), F32),
            pltpu.VMEM((40, D), F32),
            pltpu.VMEM((5, 40, 384), F32),
            pltpu.VMEM((4, 40, 384), F32),
            pltpu.VMEM((4, 40, 384), F32),
            sems((7,)), sems((7,)),
            *three,
            sems((2, 4)), sems((2, 4)),
            sems((2, 7)), sems((2, 7)),
            sems((2, 7)), sems((2, 7)),
            sems((6,)), sems((6,)),
            sems((4,)),
            sems((5,)), sems((5,)),
            sems((4, 3)), sems((4, 3)),
            *three, *three, *three,
            sems((8,)), sems((8,)),
            *three, *three,
            sems((4,)), sems((4,)),
            sems((5,)), sems((5,)),
            *three, *three, *three,
        ],
        compiler_params=pltpu.CompilerParams(
            collective_id=0, has_side_effects=True, vmem_limit_bytes=VMEM_LIMIT
        ),
        name="block",
    )(frames, dest, segment, w, gain, cot, kern, gain_m)


def tail_kernel(w_grad, small, grad_weight, g_in, g_kernel, g_mid):
    for c in range(2):
        grad_weight[:, D * c : D * c + D] = w_grad[c].astype(F32)
    g_in[...] = small[32:33, :].reshape(D)
    g_kernel[...] = small[:TAPS, :]
    g_mid[...] = small[TAPS : TAPS + 1, :].reshape(D)


def tail(w_grad, small):
    vm = pl.BlockSpec(memory_space=pltpu.VMEM)
    return pl.pallas_call(
        tail_kernel,
        out_shape=(
            jax.ShapeDtypeStruct((192, 2 * D), F32),
            jax.ShapeDtypeStruct((D,), F32),
            jax.ShapeDtypeStruct((TAPS, D), F32),
            jax.ShapeDtypeStruct((D,), F32),
        ),
        in_specs=[vm] * 2,
        out_specs=(vm,) * 4,
        name="tail",
    )(w_grad, small)


def on_device(frames_in, dest, segment, gain_in, w_glu, kernel, gain_mid, cotangent):
    output, grad_frames, w_grad, small = block(
        frames_in, dest, segment, w_glu, gain_in, cotangent, kernel, gain_mid
    )
    return (output, grad_frames, *tail(w_grad, small))


def solution(mesh):
    return jax.shard_map(
        on_device,
        mesh=mesh,
        in_specs=(
            P(("dp", "fsdp"), None),
            P(("dp", "fsdp")),
            P("dp", "fsdp"),
            P(),
            P("fsdp", None),
            P(),
            P(),
            P(("dp", "fsdp"), None),
        ),
        out_specs=(
            P(("dp", "fsdp"), None),
            P(("dp", "fsdp"), None),
            P("fsdp", None),
            P(),
            P(),
            P(),
        ),
        check_vma=False,
    )
```

```python
import jax
import jax.numpy as jnp
from jax import lax
from jax.experimental import pallas as pl
from jax.experimental.pallas import tpu as pltpu
from jax.sharding import PartitionSpec as P

EPS = 1e-05
ROWS = 384
D = 1536
TAPS = 31
MESH = pl.DeviceIdType.MESH
F32 = jnp.float32
BF16 = jnp.bfloat16
VMEM_LIMIT = 61 * 1024 * 1024


def place():
    dp = lax.axis_index("dp")
    me = lax.axis_index("fsdp")
    z_hi = lax.div(dp, 8)
    x = lax.rem(lax.div(dp, 2), 4)
    core = lax.rem(dp, 2)
    return dp, me, z_hi, x, core, lax.div(me, 2), lax.rem(me, 2)


def send(src, dst, send_sem, recv_sem, target):
    copy = pltpu.make_async_remote_copy(
        src_ref=src, dst_ref=dst, send_sem=send_sem, recv_sem=recv_sem, device_id=target, device_id_type=MESH
    )
    copy.start()
    return copy


def greet(targets):
    barrier = pltpu.get_barrier_semaphore()
    for target in targets:
        pl.semaphore_signal(barrier, inc=1, device_id=target, device_id_type=MESH)
    pl.semaphore_wait(barrier, len(targets))


def sigmoid(v):
    return 0.5 * jnp.tanh(0.5 * v) + 0.5


def vec_mean(v):
    return jnp.sum(v, axis=-1, keepdims=True) * (1.0 / D)


def block_kernel(
    frames, dest, segment, w, gain, cot, kern, gain_m,
    output, grad_frames, w_grad, small,
    packed, value, sig, gext, cext, sext, stat,
    w_all, out_buf, in_buf, normed_k, gx, mx, ex, kb, gk, seg, s1, s2,
    ncat, pcat, psend, dn, p0, p1, r0, r1, ry, rx, e0, e1, s0_in, s1_in, f, u_in, sa, sb, sy, sx, sz,
    a_s, a_r, y_s, y_r, z_s, z_r, w_s, w_r, b_s, b_r, h_s, h_r, l_s,
    c_s, c_r, q0_s, q0_r, q1_s, q1_r, m0_s, m0_r, m1_s, m1_r, u_s, u_r, v_s, v_r, x_s, x_r, d_s, d_r,
    k_s, k_r, ky_s, ky_r, kx_s, kx_r, kz_s, kz_r,
):
    dp, me, z_hi, x, core, y, z_lo = place()
    sib = (dp + 1 - 2 * core, me)
    up = (lax.rem(z_hi + z_lo, 4) * 8 + x * 2 + core, me + 1 - 2 * z_lo)
    down = (lax.rem(z_hi + 3 + z_lo, 4) * 8 + x * 2 + core, me + 1 - 2 * z_lo)
    far = (lax.rem(z_hi + 3 + 2 * z_lo, 4) * 8 + x * 2 + core, me + 1 - 2 * z_lo)
    nxt = (dp, lax.rem(me + 1, 8))
    prv = (dp, lax.rem(me + 7, 8))

    steps = (1, 3, 2)

    def x_of(s):
        return lax.rem(x + s, 4)

    def y_of(s):
        return lax.rem(y + s, 4)

    def z_of(s):
        return lax.rem(z_hi + s, 4)

    def x_dev(s):
        return (z_hi * 8 + x_of(s) * 2 + core, me)

    def y_dev(s):
        return (dp, 2 * y_of(s) + z_lo)

    def z_dev(s, same):
        return (z_of(s) * 8 + x * 2 + core, me if same else me + 1 - 2 * z_lo)

    pair = (dp, me + 1 - 2 * z_lo)
    greet(
        [(dp, lax.rem(me + s, 8)) for s in range(1, 8)]
        + [sib]
        + [x_dev(s) for s in steps]
        + [z_dev(s, True) for s in steps]
        + [z_dev(s, False) for s in steps]
    )
    sends = []

    half = core * 96
    par = lax.rem(x, 2)
    c_mine = pl.multiple_of(D * par, 128)
    c_else = pl.multiple_of(D - D * par, 128)
    c_low = pl.ds(c_mine, 768)
    c_high = pl.ds(pl.multiple_of(c_mine + 768, 128), 768)

    def rows_of(shard):
        return pl.ds(pl.multiple_of(192 * shard + half, 32), 96)

    own_rows = pl.ds(pl.multiple_of(half, 32), 96)
    y_copies = []
    for n, s in enumerate((1, 3)):
        y_copies.append(
            send(
                w.at[own_rows, pl.ds(c_mine, D)], w_all.at[rows_of(me), pl.ds(c_mine, D)],
                y_s.at[n], y_r.at[n], y_dev(s),
            )
        )
    z_copies = [
        send(w.at[own_rows, c_high], w_all.at[rows_of(me), c_high], z_s.at[0, 0], z_r.at[0, 0], up),
        send(w.at[own_rows, c_low], w_all.at[rows_of(me), c_low], z_s.at[1, 0], z_r.at[1, 0], down),
    ]
    sext[32:416, :] = jnp.broadcast_to(segment[...].astype(F32), (128, ROWS)).T.astype(jnp.int32)
    halos = [
        send(cot.at[368:384, :], cext.at[0:16, :], h_s.at[0], h_r.at[0], nxt),
        send(cot.at[0:16, :], cext.at[400:416, :], h_s.at[1], h_r.at[1], prv),
        send(sext.at[384:416, :], sext.at[0:32, :], h_s.at[2], h_r.at[2], nxt),
        send(sext.at[32:64, :], sext.at[416:448, :], h_s.at[3], h_r.at[3], prv),
    ]
    cot_copy = pltpu.make_async_copy(cot, cext.at[16:400, :], l_s.at[0])
    cot_copy.start()

    d = dest[...].reshape(1, ROWS)
    gain_in = gain[...].reshape(1, D)
    k8 = lax.broadcasted_iota(jnp.int32, (8, ROWS), 0)
    rel = d - ROWS * k8
    hot = jnp.logical_and(rel >= 0, rel < ROWS)
    hot_f = jnp.where(hot, 1.0, 0.0).astype(F32)
    before = lax.broadcasted_iota(jnp.int32, (ROWS, ROWS), 0) < lax.broadcasted_iota(jnp.int32, (ROWS, ROWS), 1)
    rank = jnp.dot(hot_f.astype(BF16), jnp.where(before, 1.0, 0.0).astype(BF16), preferred_element_type=F32)
    order = jnp.sum(hot_f * (rank + 48.0 * k8.astype(F32)), axis=0, keepdims=True)
    slot = jnp.sum(hot_f * rel.astype(F32), axis=0, keepdims=True)
    high = jnp.floor(slot * (1.0 / 16.0))
    low = slot - 16.0 * high
    row_id = lax.broadcasted_iota(jnp.int32, (ROWS, ROWS), 0).astype(F32)
    perm = jnp.where(row_id == order, 1.0, 0.0).astype(BF16)
    tag_row = lax.broadcasted_iota(jnp.int32, (128, ROWS), 0)
    tags = jnp.where(tag_row == 0, high, jnp.where(tag_row == 1, low, 0.0)).astype(BF16)
    out_buf[:, D:] = lax.dot_general(perm, tags, (((1,), (1,)), ((), ())), preferred_element_type=F32).astype(BF16)
    for c in range(3):
        out_buf[:, 512 * c : 512 * c + 512] = jnp.dot(
            perm, frames[:, 512 * c : 512 * c + 512], preferred_element_type=F32
        ).astype(BF16)
    a_copies = []
    for s in (1, 7, 2, 6, 3, 5, 4):
        peer = lax.rem(me + s, 8)
        a_copies.append(
            send(
                out_buf.at[pl.ds(48 * peer, 48), :], in_buf.at[pl.ds(48 * me, 48), :],
                a_s.at[s - 1], a_r.at[s - 1], (dp, peer),
            )
        )
    own = pltpu.make_async_copy(out_buf.at[pl.ds(48 * me, 48), :], in_buf.at[pl.ds(48 * me, 48), :], l_s.at[1])
    own.start()
    own_w = pltpu.make_async_copy(w, w_all.at[pl.ds(192 * me, 192), :], l_s.at[2])
    own_w.start()

    b_copies, w_copies = {}, {}
    shards = [2 * lax.rem(y + 4 - s, 4) + z_lo for s in steps]
    shards += [2 * lax.rem(y + 4 - t, 4) + 1 - z_lo for t in (0,) + steps]

    def pass_on(shard, index):
        rows = rows_of(shard)
        high, low_piece = w_all.at[rows, c_high], w_all.at[rows, c_low]
        w_copies[index] = [
            send(high, high, w_s.at[0, index], w_r.at[0, index], x_dev(1)),
            send(low_piece, low_piece, w_s.at[1, index], w_r.at[1, index], x_dev(3)),
        ]
        piece = w_all.at[rows, pl.ds(c_mine, D)]
        b_copies[0, index] = send(piece, piece, b_s.at[0, index], b_r.at[0, index], sib)

    def y_arrived(n, s):
        shard = shards[n]
        rows = rows_of(shard)
        high, low_piece = w_all.at[rows, c_high], w_all.at[rows, c_low]
        if n < 2:
            y_copies[n].wait_recv()
            piece = (low_piece, high)[n]
            y_copies.append(send(piece, piece, y_s.at[2 + n], y_r.at[2 + n], y_dev(s)))
        else:
            y_copies[2].wait_recv()
            y_copies[3].wait_recv()
        z_copies.append(send(high, high, z_s.at[0, s], z_r.at[0, s], up))
        z_copies.append(send(low_piece, low_piece, z_s.at[1, s], z_r.at[1, s], down))
        pass_on(shard, n)

    def z_arrived(n):
        z_copies[2 * n].wait_recv()
        z_copies[2 * n + 1].wait_recv()
        pass_on(shards[3 + n], 3 + n)

    def x_arrived(index):
        for copy in w_copies[index]:
            copy.wait_recv()
        shard = shards[index]
        piece = w_all.at[rows_of(shard), pl.ds(c_else, D)]
        b_copies[1, index] = send(piece, piece, b_s.at[1, index], b_r.at[1, index], sib)

    y_arrived(0, 1)
    y_arrived(1, 3)
    z_arrived(0)
    y_arrived(2, 2)

    own.wait()
    for copy in a_copies:
        copy.wait_recv()
    tag = in_buf[:, D:].astype(F32)
    at = tag[:, 0:1] * 16.0 + tag[:, 1:2]
    col_id = lax.broadcasted_iota(jnp.int32, (ROWS, ROWS), 1).astype(F32)
    unperm = jnp.where(col_id == at, 1.0, 0.0).T.astype(BF16)
    for c in range(3):
        packed[:, 512 * c : 512 * c + 512] = jnp.dot(
            unperm, in_buf[:, 512 * c : 512 * c + 512], preferred_element_type=F32
        ).astype(BF16)

    z_arrived(1)
    z_arrived(2)

    def norm_body(i, carry):
        rows = pl.ds(pl.multiple_of(32 * i, 32), 32)
        v = packed[rows, :].astype(F32)
        mean = vec_mean(v)
        centre = v - mean
        scale = lax.rsqrt(vec_mean(centre * centre) + EPS)
        stat[0, rows, :] = jnp.broadcast_to(mean, (32, 128))
        stat[1, rows, :] = jnp.broadcast_to(scale, (32, 128))
        unit = (centre * scale * gain_in).astype(BF16)
        psend[rows, :] = unit
        for c in range(4):
            for z in range(2):
                at = 384 * c + 192 * z
                normed_k[z, c, rows, :] = unit[:, at : at + 192]
        return carry

    lax.fori_loop(0, 12, norm_body, 0)
    z_arrived(3)
    for index in (0, 1, 3, 2):
        x_arrived(index)
    for c in range(4):
        flipped = psend[:, 384 * c : 384 * c + 384].astype(F32).T.astype(BF16)
        for z in range(2):
            for p in range(2):
                to = 768 * p + 192 * c + 96 * z
                ncat[to : to + 96, 0:384] = flipped[192 * z + 96 * p : 192 * z + 96 * p + 96, :]
    share = send(ncat.at[:, 0:384], ncat.at[:, 384:768], c_s.at[0], c_r.at[0], sib)
    sends.append(share)
    for index in (4, 5, 6):
        x_arrived(index)

    def proj(z, cols):
        total = None
        for c in range(4):
            rows = pl.ds(pl.multiple_of(384 * c + 192 * z, 64), 192)
            part = jnp.dot(normed_k[z, c], w_all[rows, cols], preferred_element_type=F32)
            total = part if total is None else total + part
        return total

    def proj_body(i, carry):
        left = pl.ds(pl.multiple_of(256 * i, 256), 256)
        right = pl.ds(pl.multiple_of(256 * i + D, 256), 256)
        value[:, left] = proj(z_lo, left)
        sig[:, left] = proj(z_lo, right)
        return carry

    def proj_rest(i, carry):
        left = pl.ds(pl.multiple_of(256 * i, 256), 256)
        right = pl.ds(pl.multiple_of(256 * i + D, 256), 256)
        v = value[:, left] + proj(1 - z_lo, left)
        s = sigmoid(sig[:, left] + proj(1 - z_lo, right))
        value[:, left] = v
        sig[:, left] = s
        gext[32:416, left] = (v * s).astype(BF16)
        return carry

    own_w.wait()
    for index in (0, 1, 2):
        b_copies[0, index].wait_recv()
        b_copies[1, index].wait_recv()
    lax.fori_loop(0, 6, proj_body, 0)
    for index in (3, 4, 5, 6):
        b_copies[0, index].wait_recv()
        b_copies[1, index].wait_recv()
    lax.fori_loop(0, 6, proj_rest, 0)
    halos.append(send(gext.at[384:416, :], gext.at[0:32, :], h_s.at[4], h_r.at[4], nxt))
    halos.append(send(gext.at[32:64, :], gext.at[416:448, :], h_s.at[5], h_r.at[5], prv))

    for l in range(12):
        cols = slice(128 * l, 128 * l + 128)
        gx[l, 32:416, :] = gext[32:416, cols].astype(F32)
        for j in range(TAPS):
            kb[l, j] = jnp.broadcast_to(kern[j : j + 1, cols], (8, 128))
    gk[...] = jnp.zeros_like(gk)
    s1[...] = jnp.zeros_like(s1)
    cot_copy.wait()
    for copy in halos:
        copy.wait_recv()
    for l in range(12):
        cols = slice(128 * l, 128 * l + 128)
        gx[l, 0:32, :] = gext[0:32, cols].astype(F32)
        gx[l, 416:448, :] = gext[416:448, cols].astype(F32)
    edge = lax.broadcasted_iota(jnp.int32, (448, 128), 0) + ROWS * me - 32
    seg[...] = jnp.where(jnp.logical_and(edge >= 0, edge < 8 * ROWS), sext[...], -1)

    def conv_block(n, carry):
        base = pl.multiple_of(32 * lax.div(n, 4), 32)
        l0 = 3 * lax.rem(n, 4)
        total = [[jnp.zeros((8, 128), F32) for _ in range(4)] for _ in range(3)]
        here = [seg[pl.ds(base + 16 + 8 * t, 8), :] for t in range(4)]
        for j in range(TAPS):
            taps = [kb[l0 + i, j] for i in range(3)]
            for t in range(4):
                at = pl.ds(base + 1 + j + 8 * t, 8)
                same = seg[at, :] == here[t]
                for i in range(3):
                    total[i][t] = total[i][t] + jnp.where(same, gx[l0 + i, at, :], 0.0) * taps[i]
        for t in range(4):
            at = pl.ds(base + 8 * t, 8)
            for i in range(3):
                mx[l0 + i, at, :] = total[i][t]
            s1[at, :] += total[0][t] + total[1][t] + total[2][t]
        return carry

    lax.fori_loop(0, 52, conv_block, 0)

    def lane_mean(v):
        return jnp.broadcast_to(jnp.sum(v, axis=-1, keepdims=True) * (1.0 / D), v.shape)

    def stat_block(i, carry):
        rows = pl.ds(pl.multiple_of(104 * i, 8), 104)
        mean = lane_mean(s1[rows, :])
        square = jnp.zeros((104, 128), F32)
        for l in range(12):
            centre = mx[l, rows, :] - mean
            mx[l, rows, :] = centre
            square = square + centre * centre
        s1[rows, :] = lax.rsqrt(lane_mean(square) + EPS)
        return carry

    lax.fori_loop(0, 4, stat_block, 0)
    gain_mid = gain_m[...].reshape(1, D)

    def gate_rows(base, size, own, acc):
        rows = pl.ds(base, size)
        scale = s1[rows, :]
        sum_e = jnp.zeros((size, 128), F32)
        sum_eu = jnp.zeros((size, 128), F32)
        sums = []
        for l in range(12):
            cols = slice(128 * l, 128 * l + 128)
            unit = mx[l, rows, :] * scale
            mid = unit * gain_mid[:, cols]
            s = sigmoid(mid)
            gated = mid * s
            d_mid = cext[rows, cols].astype(F32) * (s + gated * (1.0 - s))
            if own:
                to = pl.ds(base - 16, size)
                output[to, cols] = (packed[to, cols].astype(F32) + gated).astype(BF16)
                du = d_mid * unit
                part = acc[l]
                for t in range(size // 8):
                    part = part + du[8 * t : 8 * t + 8, :]
                sums.append(part)
            e = d_mid * gain_mid[:, cols]
            sum_e = sum_e + e
            sum_eu = sum_eu + e * unit
            mx[l, rows, :] = unit
            ex[l, rows, :] = e
        s2[0, rows, :] = sum_e
        s2[1, rows, :] = sum_eu
        return tuple(sums)

    gate_rows(0, 16, False, None)
    gate_rows(400, 16, False, None)
    gain_acc = lax.fori_loop(
        0, 12, lambda i, acc: gate_rows(pl.multiple_of(16 + 32 * i, 16), 32, True, acc),
        tuple(jnp.zeros((8, 128), F32) for _ in range(12)),
    )

    def mixed_block(i, carry):
        rows = pl.ds(pl.multiple_of(104 * i, 8), 104)
        e_mean = lane_mean(s2[0, rows, :])
        eu_mean = lane_mean(s2[1, rows, :])
        scale = s1[rows, :]
        for l in range(12):
            mx[l, rows, :] = scale * (ex[l, rows, :] - e_mean - mx[l, rows, :] * eu_mean)
        return carry

    lax.fori_loop(0, 4, mixed_block, 0)

    relay0, stage0, relay1, stage1, second0 = [None] * 4, [None] * 4, [], [], []
    turns = (2, 1, 3, 0)
    y_rows = pl.ds(pl.multiple_of(192 * y, 64), 192)

    def add_y(n):
        for copy in stage0[n]:
            copy.wait_recv()
        s = turns[n]
        cols = pl.ds(pl.multiple_of(384 * x_of(s), 128), 384)
        e0[n] = (
            p0[y_rows, cols].astype(F32)
            + r0[0, :, cols].astype(F32)
            + r0[1, :, cols].astype(F32)
        ).astype(BF16)
        if s:
            second0.append(send(e0.at[n], s0_in.at[s - 1], m0_s.at[s - 1], m0_r.at[s - 1], x_dev(s)))

    def far_y(k, offset, size):
        return pl.ds(pl.multiple_of(192 * y_of(k) + offset, 32), size)

    def relay_y(n):
        cols = pl.ds(pl.multiple_of(384 * x_of(turns[n]), 128), 384)
        for side, k, offset in ((0, 1, 0), (1, 3, 96)):
            relay0[n][side].wait_recv()
            rows = far_y(k, offset, 96)
            p0[rows, cols] = (p0[rows, cols].astype(F32) + ry[side, :, cols].astype(F32)).astype(BF16)
        stage0[n] = [
            send(p0.at[far_y(k, 0, 192), cols], r0.at[side, :, cols], q0_s.at[n, 2 + side], q0_r.at[n, 2 + side], y_dev(k))
            for side, k in ((0, 1), (1, 3))
        ]

    own_half = pl.multiple_of(D * core, 128)
    other_half = pl.multiple_of(D - D * core, 128)
    for n, s in enumerate(turns):
        q = x_of(s)
        q0 = pl.multiple_of(384 * q, 128)
        q_cols = pl.ds(q0, 384)
        l0 = 3 * q

        def back_block(b, carry, l0=l0, q0=q0):
            base = pl.multiple_of(32 * b, 32)
            total = [[jnp.zeros((8, 128), F32) for _ in range(4)] for _ in range(3)]
            glu = [[gx[l0 + i, pl.ds(base + 32 + 8 * t, 8), :] for t in range(4)] for i in range(3)]
            here = [seg[pl.ds(base + 32 + 8 * t, 8), :] for t in range(4)]
            for j in range(TAPS):
                taps = [kb[l0 + i, TAPS - 1 - j] for i in range(3)]
                grads = [None] * 3
                for t in range(4):
                    same = seg[pl.ds(base + 17 + j + 8 * t, 8), :] == here[t]
                    at = pl.ds(base + 1 + j + 8 * t, 8)
                    for i in range(3):
                        v = jnp.where(same, mx[l0 + i, at, :], 0.0)
                        total[i][t] = total[i][t] + v * taps[i]
                        grads[i] = glu[i][t] * v if t == 0 else grads[i] + glu[i][t] * v
                for i in range(3):
                    gk[l0 + i, TAPS - 1 - j] += grads[i]
            for i in range(3):
                cols = pl.ds(pl.multiple_of(q0 + 128 * i, 128), 128)
                for t in range(2):
                    rows = pl.ds(base + 16 * t, 16)
                    d_glu = jnp.concatenate([total[i][2 * t], total[i][2 * t + 1]], axis=0)
                    sg = sig[rows, cols]
                    d_value = d_glu * sg
                    d_gate = d_value * value[rows, cols] * (1.0 - sg)
                    pcat[rows, cols] = jnp.where(core == 0, d_value, d_gate).astype(BF16)
                    psend[rows, cols] = jnp.where(core == 0, d_gate, d_value).astype(BF16)
            return carry

        lax.fori_loop(0, 12, back_block, 0)
        swap = send(psend.at[:, q_cols], pcat.at[384:768, q_cols], d_s.at[n], d_r.at[n], sib)
        sends.append(swap)
        if n == 0:
            share.wait_recv()
        else:
            relay_y(n - 1)
        swap.wait_recv()

        def body0(i, carry, q_cols=q_cols):
            rows = pl.ds(pl.multiple_of(384 * i, 128), 384)
            p0[rows, q_cols] = jnp.dot(ncat[rows, :], pcat[:, q_cols], preferred_element_type=F32).astype(BF16)
            return carry

        def body1(i, carry, q=q, q_cols=q_cols):
            start = pl.multiple_of(384 * i, 128)
            p1[q, pl.ds(start, 384), :] = jnp.dot(
                ncat[pl.ds(768 + start, 384), :], pcat[:, q_cols], preferred_element_type=F32
            ).astype(BF16)
            return carry

        lax.fori_loop(0, 2, body1, 0)
        if s == 2:
            relay1 = [
                send(p1.at[q, 0:384, :], rx.at[0], q1_s.at[0], q1_r.at[0], x_dev(1)),
                send(p1.at[q, 384:768, :], rx.at[1], q1_s.at[1], q1_r.at[1], x_dev(3)),
            ]
        elif s:
            side = 0 if s == 1 else 1
            relay1[side].wait_recv()
            half_rows = slice(384 * side, 384 * side + 384)
            p1[q, half_rows, :] = (p1[q, half_rows, :].astype(F32) + rx[side].astype(F32)).astype(BF16)
            stage1.append(send(p1.at[q], r1.at[side], q1_s.at[2 + side], q1_r.at[2 + side], x_dev(s)))
        lax.fori_loop(0, 2, body0, 0)
        relay0[n] = [
            send(p0.at[far_y(2, 96 * side, 96), q_cols], ry.at[side, :, q_cols], q0_s.at[n, side], q0_r.at[n, side], y_dev(k))
            for side, k in ((0, 1), (1, 3))
        ]
        if n >= 2:
            add_y(n - 2)

    dims = (((1,), (1,)), ((), ()))

    def dn_body(i, carry):
        cols = pl.ds(pl.multiple_of(256 * i, 256), 256)
        dn[:, cols] = lax.dot_general(
            pcat[0:384, :], w_all[cols, pl.ds(own_half, D)], dims, preferred_element_type=F32
        ) + lax.dot_general(psend[...], w_all[cols, pl.ds(other_half, D)], dims, preferred_element_type=F32)
        return carry

    lax.fori_loop(0, 3, dn_body, 0)
    relay_y(3)
    add_y(2)
    lax.fori_loop(3, 6, dn_body, 0)
    add_y(3)
    for n in range(4):
        sends += relay0[n] + stage0[n]
    sends += relay1 + stage1
    for copy in stage1:
        copy.wait_recv()
    for c in range(3):
        rows_c = slice(256 * c, 256 * c + 256)
        e1[rows_c, :] = (
            p1[x, rows_c, :].astype(F32) + r1[0, rows_c, :].astype(F32) + r1[1, rows_c, :].astype(F32)
        ).astype(BF16)
    second1 = [
        send(
            e1.at[pl.ds(pl.multiple_of(192 * y_of(s), 64), 192), :], s1_in.at[s - 1],
            m1_s.at[s - 1], m1_r.at[s - 1], y_dev(s),
        )
        for s in steps
    ]

    def frames_body(i, acc):
        base = pl.multiple_of(32 * i, 32)
        rows = pl.ds(base, 32)
        mean = stat[0, rows, :]
        scale = stat[1, rows, :]
        sum_e = jnp.zeros((32, 128), F32)
        sum_eu = jnp.zeros((32, 128), F32)
        sums = []
        for l in range(12):
            cols = slice(128 * l, 128 * l + 128)
            unit = (packed[rows, cols].astype(F32) - mean) * scale
            up = dn[rows, cols]
            du = up * unit
            sums.append(acc[l] + du[0:8] + du[8:16] + du[16:24] + du[24:32])
            e = up * gain_in[:, cols]
            sum_e = sum_e + e
            sum_eu = sum_eu + e * unit
        e_mean = lane_mean(sum_e)
        eu_mean = lane_mean(sum_eu)
        for l in range(12):
            cols = slice(128 * l, 128 * l + 128)
            unit = (packed[rows, cols].astype(F32) - mean) * scale
            e = dn[rows, cols] * gain_in[:, cols]
            grad_frames[rows, cols] = (
                cext[pl.ds(base + 16, 32), cols].astype(F32) + scale * (e - e_mean - unit * eu_mean)
            ).astype(BF16)
        return tuple(sums)

    in_acc = lax.fori_loop(0, 12, frames_body, tuple(jnp.zeros((8, 128), F32) for _ in range(12)))
    for l in range(12):
        cols = slice(128 * l, 128 * l + 128)
        for j in range(TAPS):
            sa[j : j + 1, cols] = jnp.sum(gk[l, j], axis=0, keepdims=True)
        sa[TAPS : TAPS + 1, cols] = jnp.sum(gain_acc[l], axis=0, keepdims=True)
        sa[32:40, cols] = jnp.broadcast_to(jnp.sum(in_acc[l], axis=0, keepdims=True), (8, 128))

    mine = pl.multiple_of(768 * core, 128)
    other = pl.multiple_of(768 - 768 * core, 128)
    small_a = send(sa.at[:, pl.ds(other, 768)], sb.at[:, 0:768], k_s.at[0], k_r.at[0], sib)

    small_a.wait_recv()
    sb[:, 768:1536] = sb[:, 0:768] + sa[:, pl.ds(mine, 768)]
    z_mine = pl.multiple_of(768 + 384 * z_lo, 128)
    z_other = pl.multiple_of(768 + 384 - 384 * z_lo, 128)
    small_b = send(sb.at[:, pl.ds(z_other, 384)], sy.at[4], k_s.at[1], k_r.at[1], pair)
    small_b.wait_recv()
    sy[pl.ds(y, 1)] = (sb[:, pl.ds(z_mine, 384)] + sy[4])[None]
    y_small = [send(sy.at[y], sy.at[y], ky_s.at[s - 1], ky_r.at[s - 1], y_dev(s)) for s in steps]

    for copy in second0:
        copy.wait_recv()
    x_cols = pl.ds(pl.multiple_of(384 * x, 128), 384)
    sum0 = (
        e0[3].astype(F32) + s0_in[0].astype(F32) + s0_in[1].astype(F32) + s0_in[2].astype(F32)
    ).astype(BF16)
    f[0, 0:96, :] = sum0[0:96, :]
    f[1, 0:96, :] = sum0[96:192, :]
    for copy in second1:
        copy.wait_recv()
    sum1 = (
        e1[y_rows, :].astype(F32) + s1_in[0].astype(F32) + s1_in[1].astype(F32) + s1_in[2].astype(F32)
    ).astype(BF16)
    f[0, 96:192, :] = sum1[0:96, :]
    f[1, 96:192, :] = sum1[96:192, :]
    third = []
    for s in (1, 3, 2, 0):
        for same in (False, True):
            if s or not same:
                n = 2 * s + (0 if same else 1)
                zb = z_lo if same else 1 - z_lo
                third.append(
                    send(
                        f.at[zb, pl.ds(pl.multiple_of(48 * z_of(s), 16), 48), :], u_in.at[n],
                        u_s.at[n], u_r.at[n], z_dev(s, same),
                    )
                )
    for copy in y_small:
        copy.wait_recv()
    sx[pl.ds(x, 1)] = (sy[0] + sy[1] + sy[2] + sy[3])[None]
    x_small = [send(sx.at[x], sx.at[x], kx_s.at[s - 1], kx_r.at[s - 1], x_dev(s)) for s in steps]
    for copy in third:
        copy.wait_recv()

    z_rows = pl.ds(pl.multiple_of(48 * z_hi, 16), 48)
    total = f[z_lo, z_rows, :].astype(F32)
    for n in range(1, 8):
        total = total + u_in[n].astype(F32)
    w_grad[pl.ds(core, 1), z_rows, x_cols] = total.astype(BF16)[None]
    piece = w_grad.at[core, z_rows, x_cols]
    fifth = [send(piece, piece, v_s.at[s - 1], v_r.at[s - 1], z_dev(s, True)) for s in steps]
    for copy in x_small:
        copy.wait_recv()
    sz[pl.ds(z_hi, 1)] = (sx[0] + sx[1] + sx[2] + sx[3])[None]
    z_small = [send(sz.at[z_hi], sz.at[z_hi], kz_s.at[s - 1], kz_r.at[s - 1], z_dev(s, True)) for s in steps]
    for copy in fifth:
        copy.wait_recv()
    strip = w_grad.at[core, :, x_cols]
    sixth = [send(strip, strip, x_s.at[n], x_r.at[n], x_dev(s)) for n, s in ((0, 1), (1, 3))]
    seventh = [send(strip, strip, c_s.at[1], c_r.at[1], sib)]
    for copy in z_small:
        copy.wait_recv()
    col_here = pl.multiple_of(768 * core + 384 * z_lo, 128)
    small[:, pl.ds(col_here, 384)] = sz[0] + sz[1] + sz[2] + sz[3]
    here = small.at[:, pl.ds(col_here, 384)]
    small_z = send(here, here, k_s.at[2], k_r.at[2], pair)
    small_here = send(here, here, k_s.at[3], k_r.at[3], sib)
    for n, s in ((0, 1), (1, 3)):
        sixth[n].wait_recv()
        came_cols = pl.ds(pl.multiple_of(384 * x_of(4 - s), 128), 384)
        part = w_grad.at[core, 96 * n : 96 * n + 96, came_cols]
        sixth.append(send(part, part, x_s.at[2 + n], x_r.at[2 + n], x_dev(s)))
        came = w_grad.at[core, :, came_cols]
        seventh.append(send(came, came, c_s.at[2 + n], c_r.at[2 + n], sib))
    small_z.wait_recv()
    there = small.at[:, pl.ds(pl.multiple_of(768 * core + 384 - 384 * z_lo, 128), 384)]
    small_there = send(there, there, k_s.at[4], k_r.at[4], sib)
    sixth[2].wait_recv()
    sixth[3].wait_recv()
    came = w_grad.at[core, :, pl.ds(pl.multiple_of(384 * x_of(2), 128), 384)]
    seventh.append(send(came, came, c_s.at[4], c_r.at[4], sib))
    small_here.wait_recv()
    small_there.wait_recv()
    for copy in seventh:
        copy.wait_recv()
    sends += [small_a, small_b, small_z, small_here, small_there]
    sends += y_small + x_small + z_small + second0 + second1 + third + fifth + sixth + seventh
    for pair_of in w_copies.values():
        sends += pair_of
    for copy in sends + halos + a_copies + y_copies + z_copies + list(b_copies.values()):
        copy.wait_send()


def block(frames, dest, segment, w, gain, cot, kern, gain_m):
    vm = pl.BlockSpec(memory_space=pltpu.VMEM)
    hbm = pl.BlockSpec(memory_space=pl.ANY)
    sems = pltpu.SemaphoreType.DMA
    three = [sems((3,)), sems((3,))]
    return pl.pallas_call(
        block_kernel,
        out_shape=(
            jax.ShapeDtypeStruct((ROWS, D), BF16),
            jax.ShapeDtypeStruct((ROWS, D), BF16),
            jax.ShapeDtypeStruct((2, 192, D), BF16),
            jax.ShapeDtypeStruct((40, D), F32),
        ),
        in_specs=[vm, vm, vm, hbm, vm, hbm, vm, vm],
        out_specs=(vm, vm, vm, vm),
        scratch_shapes=[
            pltpu.VMEM((ROWS, D), BF16),
            pltpu.VMEM((ROWS, D), F32),
            pltpu.VMEM((ROWS, D), F32),
            pltpu.VMEM((448, D), BF16),
            pltpu.VMEM((416, D), BF16),
            pltpu.VMEM((448, 128), jnp.int32),
            pltpu.VMEM((2, ROWS, 128), F32),
            pltpu.VMEM((D, 2 * D), BF16),
            pltpu.VMEM((ROWS, D + 128), BF16),
            pltpu.VMEM((ROWS, D + 128), BF16),
            pltpu.VMEM((2, 4, ROWS, 192), BF16),
            pltpu.VMEM((12, 448, 128), F32),
            pltpu.VMEM((12, 416, 128), F32),
            pltpu.VMEM((12, 416, 128), F32),
            pltpu.VMEM((12, TAPS, 8, 128), F32),
            pltpu.VMEM((12, TAPS, 8, 128), F32),
            pltpu.VMEM((448, 128), jnp.int32),
            pltpu.VMEM((416, 128), F32),
            pltpu.VMEM((2, 416, 128), F32),
            pltpu.VMEM((D, 768), BF16),
            pltpu.VMEM((768, D), BF16),
            pltpu.VMEM((ROWS, D), BF16),
            pltpu.VMEM((ROWS, D), F32),
            pltpu.VMEM((768, D), BF16),
            pltpu.VMEM((4, 768, 384), BF16),
            pltpu.VMEM((2, 192, D), BF16),
            pltpu.VMEM((2, 768, 384), BF16),
            pltpu.VMEM((2, 96, D), BF16),
            pltpu.VMEM((2, 384, 384), BF16),
            pltpu.VMEM((4, 192, 384), BF16),
            pltpu.VMEM((768, 384), BF16),
            pltpu.VMEM((3, 192, 384), BF16),
            pltpu.VMEM((3, 192, 384), BF16),
            pltpu.VMEM((2, 192, 384), BF16),
            pltpu.VMEM((8, 48, 384), BF16),
            pltpu.VMEM((40, D), F32),
            pltpu.VMEM((40, D), F32),
            pltpu.VMEM((5, 40, 384), F32),
            pltpu.VMEM((4, 40, 384), F32),
            pltpu.VMEM((4, 40, 384), F32),
            sems((7,)), sems((7,)),
            sems((4,)), sems((4,)),
            sems((2, 4)), sems((2, 4)),
            sems((2, 7)), sems((2, 7)),
            sems((2, 7)), sems((2, 7)),
            sems((6,)), sems((6,)),
            sems((4,)),
            sems((5,)), sems((5,)),
            sems((4, 4)), sems((4, 4)),
            sems((4,)), sems((4,)),
            *three, *three,
            sems((8,)), sems((8,)),
            *three,
            sems((4,)), sems((4,)),
            sems((4,)), sems((4,)),
            sems((5,)), sems((5,)),
            *three, *three, *three,
        ],
        compiler_params=pltpu.CompilerParams(
            collective_id=0, has_side_effects=True, vmem_limit_bytes=VMEM_LIMIT
        ),
        name="block",
    )(frames, dest, segment, w, gain, cot, kern, gain_m)


def tail_kernel(w_grad, small, out_in, frames_in, grad_weight, g_in, g_kernel, g_mid, output, grad_frames, sem):
    copies = [
        pltpu.make_async_copy(out_in, output, sem.at[0]),
        pltpu.make_async_copy(frames_in, grad_frames, sem.at[1]),
    ]
    for copy in copies:
        copy.start()
    for c in range(2):
        grad_weight[:, D * c : D * c + D] = w_grad[c].astype(F32)
    g_in[...] = small[32:33, :].reshape(D)
    g_kernel[...] = small[:TAPS, :]
    g_mid[...] = small[TAPS : TAPS + 1, :].reshape(D)
    for copy in copies:
        copy.wait()


def tail(w_grad, small, output, grad_frames):
    vm = pl.BlockSpec(memory_space=pltpu.VMEM)
    hbm = pl.BlockSpec(memory_space=pl.ANY)
    return pl.pallas_call(
        tail_kernel,
        out_shape=(
            jax.ShapeDtypeStruct((192, 2 * D), F32),
            jax.ShapeDtypeStruct((D,), F32),
            jax.ShapeDtypeStruct((TAPS, D), F32),
            jax.ShapeDtypeStruct((D,), F32),
            jax.ShapeDtypeStruct((ROWS, D), BF16),
            jax.ShapeDtypeStruct((ROWS, D), BF16),
        ),
        in_specs=[vm] * 4,
        out_specs=(vm, vm, vm, vm, hbm, hbm),
        scratch_shapes=[pltpu.SemaphoreType.DMA((2,))],
        compiler_params=pltpu.CompilerParams(vmem_limit_bytes=VMEM_LIMIT),
        name="tail",
    )(w_grad, small, output, grad_frames)


def on_device(frames_in, dest, segment, gain_in, w_glu, kernel, gain_mid, cotangent):
    output, grad_frames, w_grad, small = block(
        frames_in, dest, segment, w_glu, gain_in, cotangent, kernel, gain_mid
    )
    grad_weight, g_in, g_kernel, g_mid, output, grad_frames = tail(w_grad, small, output, grad_frames)
    return (output, grad_frames, grad_weight, g_in, g_kernel, g_mid)


def solution(mesh):
    return jax.shard_map(
        on_device,
        mesh=mesh,
        in_specs=(
            P(("dp", "fsdp"), None),
            P(("dp", "fsdp")),
            P("dp", "fsdp"),
            P(),
            P("fsdp", None),
            P(),
            P(),
            P(("dp", "fsdp"), None),
        ),
        out_specs=(
            P(("dp", "fsdp"), None),
            P(("dp", "fsdp"), None),
            P("fsdp", None),
            P(),
            P(),
            P(),
        ),
        check_vma=False,
    )
```

```python
import jax
import jax.numpy as jnp
from jax import lax
from jax.experimental import pallas as pl
from jax.experimental.pallas import tpu as pltpu
from jax.sharding import PartitionSpec as P

EPS = 1e-05
ROWS = 384
D = 1536
TAPS = 31
MESH = pl.DeviceIdType.MESH
F32 = jnp.float32
BF16 = jnp.bfloat16
VMEM_LIMIT = 61 * 1024 * 1024


def place():
    dp = lax.axis_index("dp")
    me = lax.axis_index("fsdp")
    z_hi = lax.div(dp, 8)
    x = lax.rem(lax.div(dp, 2), 4)
    core = lax.rem(dp, 2)
    return dp, me, z_hi, x, core, lax.div(me, 2), lax.rem(me, 2)


def send(src, dst, send_sem, recv_sem, target):
    copy = pltpu.make_async_remote_copy(
        src_ref=src, dst_ref=dst, send_sem=send_sem, recv_sem=recv_sem, device_id=target, device_id_type=MESH
    )
    copy.start()
    return copy


def greet(targets):
    barrier = pltpu.get_barrier_semaphore()
    for target in targets:
        pl.semaphore_signal(barrier, inc=1, device_id=target, device_id_type=MESH)
    pl.semaphore_wait(barrier, len(targets))


def sigmoid(v):
    return 0.5 * jnp.tanh(0.5 * v) + 0.5


def vec_mean(v):
    return jnp.sum(v, axis=-1, keepdims=True) * (1.0 / D)


def block_kernel(
    frames_hbm, dest, segment, w, gain, cot, kern, gain_m,
    output_hbm, grad_frames_hbm, w_grad, small,
    frames, output, grad_frames, packed, value, sig, gext, cext, sext, stat,
    w_all, out_buf, in_buf, normed_k, gx, mx, ex, kb, gk, seg, s1, s2,
    ncat, pcat, psend, dn, p0, p1, r0, r1, ry, rx, e0, e1, s0_in, s1_in, f, u_in, sa, sb, sy, sx, sz,
    a_s, a_r, y_s, y_r, z_s, z_r, w_s, w_r, b_s, b_r, h_s, h_r, l_s,
    c_s, c_r, q0_s, q0_r, q1_s, q1_r, m0_s, m0_r, m1_s, m1_r, u_s, u_r, v_s, v_r, x_s, x_r, d_s, d_r,
    k_s, k_r, ky_s, ky_r, kx_s, kx_r, kz_s, kz_r,
):
    dp, me, z_hi, x, core, y, z_lo = place()
    sib = (dp + 1 - 2 * core, me)
    up = (lax.rem(z_hi + z_lo, 4) * 8 + x * 2 + core, me + 1 - 2 * z_lo)
    down = (lax.rem(z_hi + 3 + z_lo, 4) * 8 + x * 2 + core, me + 1 - 2 * z_lo)
    far = (lax.rem(z_hi + 3 + 2 * z_lo, 4) * 8 + x * 2 + core, me + 1 - 2 * z_lo)
    nxt = (dp, lax.rem(me + 1, 8))
    prv = (dp, lax.rem(me + 7, 8))

    steps = (1, 3, 2)

    def x_of(s):
        return lax.rem(x + s, 4)

    def y_of(s):
        return lax.rem(y + s, 4)

    def z_of(s):
        return lax.rem(z_hi + s, 4)

    def x_dev(s):
        return (z_hi * 8 + x_of(s) * 2 + core, me)

    def y_dev(s):
        return (dp, 2 * y_of(s) + z_lo)

    def z_dev(s, same):
        return (z_of(s) * 8 + x * 2 + core, me if same else me + 1 - 2 * z_lo)

    pair = (dp, me + 1 - 2 * z_lo)
    frames_copy = pltpu.make_async_copy(frames_hbm, frames, l_s.at[3])
    frames_copy.start()
    greet(
        [(dp, lax.rem(me + s, 8)) for s in range(1, 8)]
        + [sib]
        + [x_dev(s) for s in steps]
        + [z_dev(s, True) for s in steps]
        + [z_dev(s, False) for s in steps]
    )
    sends = []

    half = core * 96
    par = lax.rem(x, 2)
    c_mine = pl.multiple_of(D * par, 128)
    c_else = pl.multiple_of(D - D * par, 128)
    c_low = pl.ds(c_mine, 768)
    c_high = pl.ds(pl.multiple_of(c_mine + 768, 128), 768)

    def rows_of(shard):
        return pl.ds(pl.multiple_of(192 * shard + half, 32), 96)

    own_rows = pl.ds(pl.multiple_of(half, 32), 96)
    y_copies = []
    for n, s in enumerate((1, 3)):
        y_copies.append(
            send(
                w.at[own_rows, pl.ds(c_mine, D)], w_all.at[rows_of(me), pl.ds(c_mine, D)],
                y_s.at[n], y_r.at[n], y_dev(s),
            )
        )
    z_copies = [
        send(w.at[own_rows, c_high], w_all.at[rows_of(me), c_high], z_s.at[0, 0], z_r.at[0, 0], up),
        send(w.at[own_rows, c_low], w_all.at[rows_of(me), c_low], z_s.at[1, 0], z_r.at[1, 0], down),
    ]
    sext[32:416, :] = jnp.broadcast_to(segment[...].astype(F32), (128, ROWS)).T.astype(jnp.int32)
    halos = [
        send(cot.at[368:384, :], cext.at[0:16, :], h_s.at[0], h_r.at[0], nxt),
        send(cot.at[0:16, :], cext.at[400:416, :], h_s.at[1], h_r.at[1], prv),
        send(sext.at[384:416, :], sext.at[0:32, :], h_s.at[2], h_r.at[2], nxt),
        send(sext.at[32:64, :], sext.at[416:448, :], h_s.at[3], h_r.at[3], prv),
    ]
    cot_copy = pltpu.make_async_copy(cot, cext.at[16:400, :], l_s.at[0])
    cot_copy.start()

    d = dest[...].reshape(1, ROWS)
    gain_in = gain[...].reshape(1, D)
    k8 = lax.broadcasted_iota(jnp.int32, (8, ROWS), 0)
    rel = d - ROWS * k8
    hot = jnp.logical_and(rel >= 0, rel < ROWS)
    hot_f = jnp.where(hot, 1.0, 0.0).astype(F32)
    before = lax.broadcasted_iota(jnp.int32, (ROWS, ROWS), 0) < lax.broadcasted_iota(jnp.int32, (ROWS, ROWS), 1)
    rank = jnp.dot(hot_f.astype(BF16), jnp.where(before, 1.0, 0.0).astype(BF16), preferred_element_type=F32)
    order = jnp.sum(hot_f * (rank + 48.0 * k8.astype(F32)), axis=0, keepdims=True)
    slot = jnp.sum(hot_f * rel.astype(F32), axis=0, keepdims=True)
    high = jnp.floor(slot * (1.0 / 16.0))
    low = slot - 16.0 * high
    row_id = lax.broadcasted_iota(jnp.int32, (ROWS, ROWS), 0).astype(F32)
    perm = jnp.where(row_id == order, 1.0, 0.0).astype(BF16)
    tag_row = lax.broadcasted_iota(jnp.int32, (128, ROWS), 0)
    tags = jnp.where(tag_row == 0, high, jnp.where(tag_row == 1, low, 0.0)).astype(BF16)
    out_buf[:, D:] = lax.dot_general(perm, tags, (((1,), (1,)), ((), ())), preferred_element_type=F32).astype(BF16)
    frames_copy.wait()
    for c in range(3):
        out_buf[:, 512 * c : 512 * c + 512] = jnp.dot(
            perm, frames[:, 512 * c : 512 * c + 512], preferred_element_type=F32
        ).astype(BF16)
    a_copies = []
    for s in (1, 7, 2, 6, 3, 5, 4):
        peer = lax.rem(me + s, 8)
        a_copies.append(
            send(
                out_buf.at[pl.ds(48 * peer, 48), :], in_buf.at[pl.ds(48 * me, 48), :],
                a_s.at[s - 1], a_r.at[s - 1], (dp, peer),
            )
        )
    own = pltpu.make_async_copy(out_buf.at[pl.ds(48 * me, 48), :], in_buf.at[pl.ds(48 * me, 48), :], l_s.at[1])
    own.start()
    own_w = pltpu.make_async_copy(w, w_all.at[pl.ds(192 * me, 192), :], l_s.at[2])
    own_w.start()

    b_copies, w_copies = {}, {}
    shards = [2 * lax.rem(y + 4 - s, 4) + z_lo for s in steps]
    shards += [2 * lax.rem(y + 4 - t, 4) + 1 - z_lo for t in (0,) + steps]

    def pass_on(shard, index):
        rows = rows_of(shard)
        high, low_piece = w_all.at[rows, c_high], w_all.at[rows, c_low]
        w_copies[index] = [
            send(high, high, w_s.at[0, index], w_r.at[0, index], x_dev(1)),
            send(low_piece, low_piece, w_s.at[1, index], w_r.at[1, index], x_dev(3)),
        ]
        piece = w_all.at[rows, pl.ds(c_mine, D)]
        b_copies[0, index] = send(piece, piece, b_s.at[0, index], b_r.at[0, index], sib)

    def y_arrived(n, s):
        shard = shards[n]
        rows = rows_of(shard)
        high, low_piece = w_all.at[rows, c_high], w_all.at[rows, c_low]
        if n < 2:
            y_copies[n].wait_recv()
            piece = (low_piece, high)[n]
            y_copies.append(send(piece, piece, y_s.at[2 + n], y_r.at[2 + n], y_dev(s)))
        else:
            y_copies[2].wait_recv()
            y_copies[3].wait_recv()
        z_copies.append(send(high, high, z_s.at[0, s], z_r.at[0, s], up))
        z_copies.append(send(low_piece, low_piece, z_s.at[1, s], z_r.at[1, s], down))
        pass_on(shard, n)

    def z_arrived(n):
        z_copies[2 * n].wait_recv()
        z_copies[2 * n + 1].wait_recv()
        pass_on(shards[3 + n], 3 + n)

    def x_arrived(index):
        for copy in w_copies[index]:
            copy.wait_recv()
        shard = shards[index]
        piece = w_all.at[rows_of(shard), pl.ds(c_else, D)]
        b_copies[1, index] = send(piece, piece, b_s.at[1, index], b_r.at[1, index], sib)

    y_arrived(0, 1)
    y_arrived(1, 3)
    z_arrived(0)
    y_arrived(2, 2)

    own.wait()
    for copy in a_copies:
        copy.wait_recv()
    tag = in_buf[:, D:].astype(F32)
    at = tag[:, 0:1] * 16.0 + tag[:, 1:2]
    col_id = lax.broadcasted_iota(jnp.int32, (ROWS, ROWS), 1).astype(F32)
    unperm = jnp.where(col_id == at, 1.0, 0.0).T.astype(BF16)
    for c in range(3):
        packed[:, 512 * c : 512 * c + 512] = jnp.dot(
            unperm, in_buf[:, 512 * c : 512 * c + 512], preferred_element_type=F32
        ).astype(BF16)

    z_arrived(1)
    z_arrived(2)

    def norm_body(i, carry):
        rows = pl.ds(pl.multiple_of(32 * i, 32), 32)
        v = packed[rows, :].astype(F32)
        mean = vec_mean(v)
        centre = v - mean
        scale = lax.rsqrt(vec_mean(centre * centre) + EPS)
        stat[0, rows, :] = jnp.broadcast_to(mean, (32, 128))
        stat[1, rows, :] = jnp.broadcast_to(scale, (32, 128))
        unit = (centre * scale * gain_in).astype(BF16)
        psend[rows, :] = unit
        for c in range(4):
            for z in range(2):
                at = 384 * c + 192 * z
                normed_k[z, c, rows, :] = unit[:, at : at + 192]
        return carry

    lax.fori_loop(0, 12, norm_body, 0)
    z_arrived(3)
    for index in (0, 1, 3, 2):
        x_arrived(index)
    for c in range(4):
        flipped = psend[:, 384 * c : 384 * c + 384].astype(F32).T.astype(BF16)
        for z in range(2):
            for p in range(2):
                to = 768 * p + 192 * c + 96 * z
                ncat[to : to + 96, 0:384] = flipped[192 * z + 96 * p : 192 * z + 96 * p + 96, :]
    share = send(ncat.at[:, 0:384], ncat.at[:, 384:768], c_s.at[0], c_r.at[0], sib)
    sends.append(share)
    for index in (4, 5, 6):
        x_arrived(index)

    def proj(z, cols):
        total = None
        for c in range(4):
            rows = pl.ds(pl.multiple_of(384 * c + 192 * z, 64), 192)
            part = jnp.dot(normed_k[z, c], w_all[rows, cols], preferred_element_type=F32)
            total = part if total is None else total + part
        return total

    def proj_body(i, carry):
        left = pl.ds(pl.multiple_of(256 * i, 256), 256)
        right = pl.ds(pl.multiple_of(256 * i + D, 256), 256)
        value[:, left] = proj(z_lo, left)
        sig[:, left] = proj(z_lo, right)
        return carry

    def proj_rest(i, carry):
        left = pl.ds(pl.multiple_of(256 * i, 256), 256)
        right = pl.ds(pl.multiple_of(256 * i + D, 256), 256)
        v = value[:, left] + proj(1 - z_lo, left)
        s = sigmoid(sig[:, left] + proj(1 - z_lo, right))
        value[:, left] = v
        sig[:, left] = s
        gext[32:416, left] = (v * s).astype(BF16)
        return carry

    own_w.wait()
    for index in (0, 1, 2):
        b_copies[0, index].wait_recv()
        b_copies[1, index].wait_recv()
    lax.fori_loop(0, 6, proj_body, 0)
    for index in (3, 4, 5, 6):
        b_copies[0, index].wait_recv()
        b_copies[1, index].wait_recv()
    lax.fori_loop(0, 6, proj_rest, 0)
    halos.append(send(gext.at[384:416, :], gext.at[0:32, :], h_s.at[4], h_r.at[4], nxt))
    halos.append(send(gext.at[32:64, :], gext.at[416:448, :], h_s.at[5], h_r.at[5], prv))

    for l in range(12):
        cols = slice(128 * l, 128 * l + 128)
        gx[l, 32:416, :] = gext[32:416, cols].astype(F32)
        for j in range(TAPS):
            kb[l, j] = jnp.broadcast_to(kern[j : j + 1, cols], (8, 128))
    gk[...] = jnp.zeros_like(gk)
    s1[...] = jnp.zeros_like(s1)
    cot_copy.wait()
    for copy in halos:
        copy.wait_recv()
    for l in range(12):
        cols = slice(128 * l, 128 * l + 128)
        gx[l, 0:32, :] = gext[0:32, cols].astype(F32)
        gx[l, 416:448, :] = gext[416:448, cols].astype(F32)
    edge = lax.broadcasted_iota(jnp.int32, (448, 128), 0) + ROWS * me - 32
    seg[...] = jnp.where(jnp.logical_and(edge >= 0, edge < 8 * ROWS), sext[...], -1)

    def conv_block(n, carry):
        base = pl.multiple_of(32 * lax.div(n, 4), 32)
        l0 = 3 * lax.rem(n, 4)
        total = [[jnp.zeros((8, 128), F32) for _ in range(4)] for _ in range(3)]
        here = [seg[pl.ds(base + 16 + 8 * t, 8), :] for t in range(4)]
        for j in range(TAPS):
            taps = [kb[l0 + i, j] for i in range(3)]
            for t in range(4):
                at = pl.ds(base + 1 + j + 8 * t, 8)
                same = seg[at, :] == here[t]
                for i in range(3):
                    total[i][t] = total[i][t] + jnp.where(same, gx[l0 + i, at, :], 0.0) * taps[i]
        for t in range(4):
            at = pl.ds(base + 8 * t, 8)
            for i in range(3):
                mx[l0 + i, at, :] = total[i][t]
            s1[at, :] += total[0][t] + total[1][t] + total[2][t]
        return carry

    lax.fori_loop(0, 52, conv_block, 0)

    def lane_mean(v):
        return jnp.broadcast_to(jnp.sum(v, axis=-1, keepdims=True) * (1.0 / D), v.shape)

    def stat_block(i, carry):
        rows = pl.ds(pl.multiple_of(104 * i, 8), 104)
        mean = lane_mean(s1[rows, :])
        square = jnp.zeros((104, 128), F32)
        for l in range(12):
            centre = mx[l, rows, :] - mean
            mx[l, rows, :] = centre
            square = square + centre * centre
        s1[rows, :] = lax.rsqrt(lane_mean(square) + EPS)
        return carry

    lax.fori_loop(0, 4, stat_block, 0)
    gain_mid = gain_m[...].reshape(1, D)

    def gate_rows(base, size, own, acc):
        rows = pl.ds(base, size)
        scale = s1[rows, :]
        sum_e = jnp.zeros((size, 128), F32)
        sum_eu = jnp.zeros((size, 128), F32)
        sums = []
        for l in range(12):
            cols = slice(128 * l, 128 * l + 128)
            unit = mx[l, rows, :] * scale
            mid = unit * gain_mid[:, cols]
            s = sigmoid(mid)
            gated = mid * s
            d_mid = cext[rows, cols].astype(F32) * (s + gated * (1.0 - s))
            if own:
                to = pl.ds(base - 16, size)
                output[to, cols] = (packed[to, cols].astype(F32) + gated).astype(BF16)
                du = d_mid * unit
                part = acc[l]
                for t in range(size // 8):
                    part = part + du[8 * t : 8 * t + 8, :]
                sums.append(part)
            e = d_mid * gain_mid[:, cols]
            sum_e = sum_e + e
            sum_eu = sum_eu + e * unit
            mx[l, rows, :] = unit
            ex[l, rows, :] = e
        s2[0, rows, :] = sum_e
        s2[1, rows, :] = sum_eu
        return tuple(sums)

    gate_rows(0, 16, False, None)
    gate_rows(400, 16, False, None)
    gain_acc = lax.fori_loop(
        0, 12, lambda i, acc: gate_rows(pl.multiple_of(16 + 32 * i, 16), 32, True, acc),
        tuple(jnp.zeros((8, 128), F32) for _ in range(12)),
    )

    output_copy = pltpu.make_async_copy(output, output_hbm, l_s.at[4])
    output_copy.start()

    def mixed_block(i, carry):
        rows = pl.ds(pl.multiple_of(104 * i, 8), 104)
        e_mean = lane_mean(s2[0, rows, :])
        eu_mean = lane_mean(s2[1, rows, :])
        scale = s1[rows, :]
        for l in range(12):
            mx[l, rows, :] = scale * (ex[l, rows, :] - e_mean - mx[l, rows, :] * eu_mean)
        return carry

    lax.fori_loop(0, 4, mixed_block, 0)

    relay0, stage0, relay1, stage1, second0 = [None] * 4, [None] * 4, [], [], []
    turns = (2, 1, 3, 0)
    y_rows = pl.ds(pl.multiple_of(192 * y, 64), 192)

    def add_y(n):
        for copy in stage0[n]:
            copy.wait_recv()
        s = turns[n]
        cols = pl.ds(pl.multiple_of(384 * x_of(s), 128), 384)
        e0[n] = (
            p0[y_rows, cols].astype(F32)
            + r0[0, :, cols].astype(F32)
            + r0[1, :, cols].astype(F32)
        ).astype(BF16)
        if s:
            second0.append(send(e0.at[n], s0_in.at[s - 1], m0_s.at[s - 1], m0_r.at[s - 1], x_dev(s)))

    def far_y(k, offset, size):
        return pl.ds(pl.multiple_of(192 * y_of(k) + offset, 32), size)

    def relay_y(n):
        cols = pl.ds(pl.multiple_of(384 * x_of(turns[n]), 128), 384)
        for side, k, offset in ((0, 1, 0), (1, 3, 96)):
            relay0[n][side].wait_recv()
            rows = far_y(k, offset, 96)
            p0[rows, cols] = (p0[rows, cols].astype(F32) + ry[side, :, cols].astype(F32)).astype(BF16)
        stage0[n] = [
            send(p0.at[far_y(k, 0, 192), cols], r0.at[side, :, cols], q0_s.at[n, 2 + side], q0_r.at[n, 2 + side], y_dev(k))
            for side, k in ((0, 1), (1, 3))
        ]

    own_half = pl.multiple_of(D * core, 128)
    other_half = pl.multiple_of(D - D * core, 128)
    for n, s in enumerate(turns):
        q = x_of(s)
        q0 = pl.multiple_of(384 * q, 128)
        q_cols = pl.ds(q0, 384)
        l0 = 3 * q

        def back_block(b, carry, l0=l0, q0=q0):
            base = pl.multiple_of(32 * b, 32)
            total = [[jnp.zeros((8, 128), F32) for _ in range(4)] for _ in range(3)]
            glu = [[gx[l0 + i, pl.ds(base + 32 + 8 * t, 8), :] for t in range(4)] for i in range(3)]
            here = [seg[pl.ds(base + 32 + 8 * t, 8), :] for t in range(4)]
            for j in range(TAPS):
                taps = [kb[l0 + i, TAPS - 1 - j] for i in range(3)]
                grads = [None] * 3
                for t in range(4):
                    same = seg[pl.ds(base + 17 + j + 8 * t, 8), :] == here[t]
                    at = pl.ds(base + 1 + j + 8 * t, 8)
                    for i in range(3):
                        v = jnp.where(same, mx[l0 + i, at, :], 0.0)
                        total[i][t] = total[i][t] + v * taps[i]
                        grads[i] = glu[i][t] * v if t == 0 else grads[i] + glu[i][t] * v
                for i in range(3):
                    gk[l0 + i, TAPS - 1 - j] += grads[i]
            for i in range(3):
                cols = pl.ds(pl.multiple_of(q0 + 128 * i, 128), 128)
                for t in range(2):
                    rows = pl.ds(base + 16 * t, 16)
                    d_glu = jnp.concatenate([total[i][2 * t], total[i][2 * t + 1]], axis=0)
                    sg = sig[rows, cols]
                    d_value = d_glu * sg
                    d_gate = d_value * value[rows, cols] * (1.0 - sg)
                    pcat[rows, cols] = jnp.where(core == 0, d_value, d_gate).astype(BF16)
                    psend[rows, cols] = jnp.where(core == 0, d_gate, d_value).astype(BF16)
            return carry

        lax.fori_loop(0, 12, back_block, 0)
        swap = send(psend.at[:, q_cols], pcat.at[384:768, q_cols], d_s.at[n], d_r.at[n], sib)
        sends.append(swap)
        if n == 0:
            share.wait_recv()
        else:
            relay_y(n - 1)
        swap.wait_recv()

        def body0(i, carry, q_cols=q_cols):
            rows = pl.ds(pl.multiple_of(384 * i, 128), 384)
            p0[rows, q_cols] = jnp.dot(ncat[rows, :], pcat[:, q_cols], preferred_element_type=F32).astype(BF16)
            return carry

        def body1(i, carry, q=q, q_cols=q_cols):
            start = pl.multiple_of(384 * i, 128)
            p1[q, pl.ds(start, 384), :] = jnp.dot(
                ncat[pl.ds(768 + start, 384), :], pcat[:, q_cols], preferred_element_type=F32
            ).astype(BF16)
            return carry

        lax.fori_loop(0, 2, body1, 0)
        if s == 2:
            relay1 = [
                send(p1.at[q, 0:384, :], rx.at[0], q1_s.at[0], q1_r.at[0], x_dev(1)),
                send(p1.at[q, 384:768, :], rx.at[1], q1_s.at[1], q1_r.at[1], x_dev(3)),
            ]
        elif s:
            side = 0 if s == 1 else 1
            relay1[side].wait_recv()
            half_rows = slice(384 * side, 384 * side + 384)
            p1[q, half_rows, :] = (p1[q, half_rows, :].astype(F32) + rx[side].astype(F32)).astype(BF16)
            stage1.append(send(p1.at[q], r1.at[side], q1_s.at[2 + side], q1_r.at[2 + side], x_dev(s)))
        lax.fori_loop(0, 2, body0, 0)
        relay0[n] = [
            send(p0.at[far_y(2, 96 * side, 96), q_cols], ry.at[side, :, q_cols], q0_s.at[n, side], q0_r.at[n, side], y_dev(k))
            for side, k in ((0, 1), (1, 3))
        ]
        if n >= 2:
            add_y(n - 2)

    dims = (((1,), (1,)), ((), ()))

    def dn_body(i, carry):
        cols = pl.ds(pl.multiple_of(256 * i, 256), 256)
        dn[:, cols] = lax.dot_general(
            pcat[0:384, :], w_all[cols, pl.ds(own_half, D)], dims, preferred_element_type=F32
        ) + lax.dot_general(psend[...], w_all[cols, pl.ds(other_half, D)], dims, preferred_element_type=F32)
        return carry

    lax.fori_loop(0, 3, dn_body, 0)
    relay_y(3)
    add_y(2)
    lax.fori_loop(3, 6, dn_body, 0)
    add_y(3)
    for n in range(4):
        sends += relay0[n] + stage0[n]
    sends += relay1 + stage1
    for copy in stage1:
        copy.wait_recv()
    for c in range(3):
        rows_c = slice(256 * c, 256 * c + 256)
        e1[rows_c, :] = (
            p1[x, rows_c, :].astype(F32) + r1[0, rows_c, :].astype(F32) + r1[1, rows_c, :].astype(F32)
        ).astype(BF16)
    second1 = [
        send(
            e1.at[pl.ds(pl.multiple_of(192 * y_of(s), 64), 192), :], s1_in.at[s - 1],
            m1_s.at[s - 1], m1_r.at[s - 1], y_dev(s),
        )
        for s in steps
    ]

    def frames_body(i, acc):
        base = pl.multiple_of(32 * i, 32)
        rows = pl.ds(base, 32)
        mean = stat[0, rows, :]
        scale = stat[1, rows, :]
        sum_e = jnp.zeros((32, 128), F32)
        sum_eu = jnp.zeros((32, 128), F32)
        sums = []
        for l in range(12):
            cols = slice(128 * l, 128 * l + 128)
            unit = (packed[rows, cols].astype(F32) - mean) * scale
            up = dn[rows, cols]
            du = up * unit
            sums.append(acc[l] + du[0:8] + du[8:16] + du[16:24] + du[24:32])
            e = up * gain_in[:, cols]
            sum_e = sum_e + e
            sum_eu = sum_eu + e * unit
        e_mean = lane_mean(sum_e)
        eu_mean = lane_mean(sum_eu)
        for l in range(12):
            cols = slice(128 * l, 128 * l + 128)
            unit = (packed[rows, cols].astype(F32) - mean) * scale
            e = dn[rows, cols] * gain_in[:, cols]
            grad_frames[rows, cols] = (
                cext[pl.ds(base + 16, 32), cols].astype(F32) + scale * (e - e_mean - unit * eu_mean)
            ).astype(BF16)
        return tuple(sums)

    in_acc = lax.fori_loop(0, 12, frames_body, tuple(jnp.zeros((8, 128), F32) for _ in range(12)))
    grad_frames_copy = pltpu.make_async_copy(grad_frames, grad_frames_hbm, l_s.at[5])
    grad_frames_copy.start()
    for l in range(12):
        cols = slice(128 * l, 128 * l + 128)
        for j in range(TAPS):
            sa[j : j + 1, cols] = jnp.sum(gk[l, j], axis=0, keepdims=True)
        sa[TAPS : TAPS + 1, cols] = jnp.sum(gain_acc[l], axis=0, keepdims=True)
        sa[32:40, cols] = jnp.broadcast_to(jnp.sum(in_acc[l], axis=0, keepdims=True), (8, 128))

    mine = pl.multiple_of(768 * core, 128)
    other = pl.multiple_of(768 - 768 * core, 128)
    small_a = send(sa.at[:, pl.ds(other, 768)], sb.at[:, 0:768], k_s.at[0], k_r.at[0], sib)

    small_a.wait_recv()
    sb[:, 768:1536] = sb[:, 0:768] + sa[:, pl.ds(mine, 768)]
    z_mine = pl.multiple_of(768 + 384 * z_lo, 128)
    z_other = pl.multiple_of(768 + 384 - 384 * z_lo, 128)
    small_b = send(sb.at[:, pl.ds(z_other, 384)], sy.at[4], k_s.at[1], k_r.at[1], pair)
    small_b.wait_recv()
    sy[pl.ds(y, 1)] = (sb[:, pl.ds(z_mine, 384)] + sy[4])[None]
    y_small = [send(sy.at[y], sy.at[y], ky_s.at[s - 1], ky_r.at[s - 1], y_dev(s)) for s in steps]

    for copy in second0:
        copy.wait_recv()
    x_cols = pl.ds(pl.multiple_of(384 * x, 128), 384)
    sum0 = (
        e0[3].astype(F32) + s0_in[0].astype(F32) + s0_in[1].astype(F32) + s0_in[2].astype(F32)
    ).astype(BF16)
    f[0, 0:96, :] = sum0[0:96, :]
    f[1, 0:96, :] = sum0[96:192, :]
    for copy in second1:
        copy.wait_recv()
    sum1 = (
        e1[y_rows, :].astype(F32) + s1_in[0].astype(F32) + s1_in[1].astype(F32) + s1_in[2].astype(F32)
    ).astype(BF16)
    f[0, 96:192, :] = sum1[0:96, :]
    f[1, 96:192, :] = sum1[96:192, :]
    third = []
    for s in (1, 3, 2, 0):
        for same in (False, True):
            if s or not same:
                n = 2 * s + (0 if same else 1)
                zb = z_lo if same else 1 - z_lo
                third.append(
                    send(
                        f.at[zb, pl.ds(pl.multiple_of(48 * z_of(s), 16), 48), :], u_in.at[n],
                        u_s.at[n], u_r.at[n], z_dev(s, same),
                    )
                )
    for copy in y_small:
        copy.wait_recv()
    sx[pl.ds(x, 1)] = (sy[0] + sy[1] + sy[2] + sy[3])[None]
    x_small = [send(sx.at[x], sx.at[x], kx_s.at[s - 1], kx_r.at[s - 1], x_dev(s)) for s in steps]
    for copy in third:
        copy.wait_recv()

    z_rows = pl.ds(pl.multiple_of(48 * z_hi, 16), 48)
    total = f[z_lo, z_rows, :].astype(F32)
    for n in range(1, 8):
        total = total + u_in[n].astype(F32)
    w_grad[pl.ds(core, 1), z_rows, x_cols] = total.astype(BF16)[None]
    piece = w_grad.at[core, z_rows, x_cols]
    fifth = [send(piece, piece, v_s.at[s - 1], v_r.at[s - 1], z_dev(s, True)) for s in steps]
    for copy in x_small:
        copy.wait_recv()
    sz[pl.ds(z_hi, 1)] = (sx[0] + sx[1] + sx[2] + sx[3])[None]
    z_small = [send(sz.at[z_hi], sz.at[z_hi], kz_s.at[s - 1], kz_r.at[s - 1], z_dev(s, True)) for s in steps]
    for copy in fifth:
        copy.wait_recv()
    strip = w_grad.at[core, :, x_cols]
    sixth = [send(strip, strip, x_s.at[n], x_r.at[n], x_dev(s)) for n, s in ((0, 1), (1, 3))]
    seventh = [send(strip, strip, c_s.at[1], c_r.at[1], sib)]
    for copy in z_small:
        copy.wait_recv()
    col_here = pl.multiple_of(768 * core + 384 * z_lo, 128)
    small[:, pl.ds(col_here, 384)] = sz[0] + sz[1] + sz[2] + sz[3]
    here = small.at[:, pl.ds(col_here, 384)]
    small_z = send(here, here, k_s.at[2], k_r.at[2], pair)
    small_here = send(here, here, k_s.at[3], k_r.at[3], sib)
    for n, s in ((0, 1), (1, 3)):
        sixth[n].wait_recv()
        came_cols = pl.ds(pl.multiple_of(384 * x_of(4 - s), 128), 384)
        part = w_grad.at[core, 96 * n : 96 * n + 96, came_cols]
        sixth.append(send(part, part, x_s.at[2 + n], x_r.at[2 + n], x_dev(s)))
        came = w_grad.at[core, :, came_cols]
        seventh.append(send(came, came, c_s.at[2 + n], c_r.at[2 + n], sib))
    small_z.wait_recv()
    there = small.at[:, pl.ds(pl.multiple_of(768 * core + 384 - 384 * z_lo, 128), 384)]
    small_there = send(there, there, k_s.at[4], k_r.at[4], sib)
    sixth[2].wait_recv()
    sixth[3].wait_recv()
    came = w_grad.at[core, :, pl.ds(pl.multiple_of(384 * x_of(2), 128), 384)]
    seventh.append(send(came, came, c_s.at[4], c_r.at[4], sib))
    small_here.wait_recv()
    small_there.wait_recv()
    for copy in seventh:
        copy.wait_recv()
    sends += [small_a, small_b, small_z, small_here, small_there]
    sends += y_small + x_small + z_small + second0 + second1 + third + fifth + sixth + seventh
    output_copy.wait()
    grad_frames_copy.wait()
    for pair_of in w_copies.values():
        sends += pair_of
    for copy in sends + halos + a_copies + y_copies + z_copies + list(b_copies.values()):
        copy.wait_send()


def block(frames, dest, segment, w, gain, cot, kern, gain_m):
    vm = pl.BlockSpec(memory_space=pltpu.VMEM)
    hbm = pl.BlockSpec(memory_space=pl.ANY)
    sems = pltpu.SemaphoreType.DMA
    three = [sems((3,)), sems((3,))]
    return pl.pallas_call(
        block_kernel,
        out_shape=(
            jax.ShapeDtypeStruct((ROWS, D), BF16),
            jax.ShapeDtypeStruct((ROWS, D), BF16),
            jax.ShapeDtypeStruct((2, 192, D), BF16),
            jax.ShapeDtypeStruct((40, D), F32),
        ),
        in_specs=[hbm, vm, vm, hbm, vm, hbm, vm, vm],
        out_specs=(hbm, hbm, vm, vm),
        scratch_shapes=[
            pltpu.VMEM((ROWS, D), BF16),
            pltpu.VMEM((ROWS, D), BF16),
            pltpu.VMEM((ROWS, D), BF16),
            pltpu.VMEM((ROWS, D), BF16),
            pltpu.VMEM((ROWS, D), F32),
            pltpu.VMEM((ROWS, D), F32),
            pltpu.VMEM((448, D), BF16),
            pltpu.VMEM((416, D), BF16),
            pltpu.VMEM((448, 128), jnp.int32),
            pltpu.VMEM((2, ROWS, 128), F32),
            pltpu.VMEM((D, 2 * D), BF16),
            pltpu.VMEM((ROWS, D + 128), BF16),
            pltpu.VMEM((ROWS, D + 128), BF16),
            pltpu.VMEM((2, 4, ROWS, 192), BF16),
            pltpu.VMEM((12, 448, 128), F32),
            pltpu.VMEM((12, 416, 128), F32),
            pltpu.VMEM((12, 416, 128), F32),
            pltpu.VMEM((12, TAPS, 8, 128), F32),
            pltpu.VMEM((12, TAPS, 8, 128), F32),
            pltpu.VMEM((448, 128), jnp.int32),
            pltpu.VMEM((416, 128), F32),
            pltpu.VMEM((2, 416, 128), F32),
            pltpu.VMEM((D, 768), BF16),
            pltpu.VMEM((768, D), BF16),
            pltpu.VMEM((ROWS, D), BF16),
            pltpu.VMEM((ROWS, D), F32),
            pltpu.VMEM((768, D), BF16),
            pltpu.VMEM((4, 768, 384), BF16),
            pltpu.VMEM((2, 192, D), BF16),
            pltpu.VMEM((2, 768, 384), BF16),
            pltpu.VMEM((2, 96, D), BF16),
            pltpu.VMEM((2, 384, 384), BF16),
            pltpu.VMEM((4, 192, 384), BF16),
            pltpu.VMEM((768, 384), BF16),
            pltpu.VMEM((3, 192, 384), BF16),
            pltpu.VMEM((3, 192, 384), BF16),
            pltpu.VMEM((2, 192, 384), BF16),
            pltpu.VMEM((8, 48, 384), BF16),
            pltpu.VMEM((40, D), F32),
            pltpu.VMEM((40, D), F32),
            pltpu.VMEM((5, 40, 384), F32),
            pltpu.VMEM((4, 40, 384), F32),
            pltpu.VMEM((4, 40, 384), F32),
            sems((7,)), sems((7,)),
            sems((4,)), sems((4,)),
            sems((2, 4)), sems((2, 4)),
            sems((2, 7)), sems((2, 7)),
            sems((2, 7)), sems((2, 7)),
            sems((6,)), sems((6,)),
            sems((6,)),
            sems((5,)), sems((5,)),
            sems((4, 4)), sems((4, 4)),
            sems((4,)), sems((4,)),
            *three, *three,
            sems((8,)), sems((8,)),
            *three,
            sems((4,)), sems((4,)),
            sems((4,)), sems((4,)),
            sems((5,)), sems((5,)),
            *three, *three, *three,
        ],
        compiler_params=pltpu.CompilerParams(
            collective_id=0, has_side_effects=True, vmem_limit_bytes=VMEM_LIMIT
        ),
        name="block",
    )(frames, dest, segment, w, gain, cot, kern, gain_m)


def tail_kernel(w_grad, small, out_in, frames_in, grad_weight, g_in, g_kernel, g_mid, output, grad_frames, sem):
    copies = [
        pltpu.make_async_copy(out_in, output, sem.at[0]),
        pltpu.make_async_copy(frames_in, grad_frames, sem.at[1]),
    ]
    for copy in copies:
        copy.start()
    for c in range(2):
        grad_weight[:, D * c : D * c + D] = w_grad[c].astype(F32)
    g_in[...] = small[32:33, :].reshape(D)
    g_kernel[...] = small[:TAPS, :]
    g_mid[...] = small[TAPS : TAPS + 1, :].reshape(D)
    for copy in copies:
        copy.wait()


def tail(w_grad, small, output, grad_frames):
    vm = pl.BlockSpec(memory_space=pltpu.VMEM)
    hbm = pl.BlockSpec(memory_space=pl.ANY)
    return pl.pallas_call(
        tail_kernel,
        out_shape=(
            jax.ShapeDtypeStruct((192, 2 * D), F32),
            jax.ShapeDtypeStruct((D,), F32),
            jax.ShapeDtypeStruct((TAPS, D), F32),
            jax.ShapeDtypeStruct((D,), F32),
            jax.ShapeDtypeStruct((ROWS, D), BF16),
            jax.ShapeDtypeStruct((ROWS, D), BF16),
        ),
        in_specs=[vm] * 4,
        out_specs=(vm, vm, vm, vm, hbm, hbm),
        scratch_shapes=[pltpu.SemaphoreType.DMA((2,))],
        compiler_params=pltpu.CompilerParams(vmem_limit_bytes=VMEM_LIMIT),
        name="tail",
    )(w_grad, small, output, grad_frames)


def on_device(frames_in, dest, segment, gain_in, w_glu, kernel, gain_mid, cotangent):
    output, grad_frames, w_grad, small = block(
        frames_in, dest, segment, w_glu, gain_in, cotangent, kernel, gain_mid
    )
    grad_weight, g_in, g_kernel, g_mid, output, grad_frames = tail(w_grad, small, output, grad_frames)
    return (output, grad_frames, grad_weight, g_in, g_kernel, g_mid)


def solution(mesh):
    return jax.shard_map(
        on_device,
        mesh=mesh,
        in_specs=(
            P(("dp", "fsdp"), None),
            P(("dp", "fsdp")),
            P("dp", "fsdp"),
            P(),
            P("fsdp", None),
            P(),
            P(),
            P(("dp", "fsdp"), None),
        ),
        out_specs=(
            P(("dp", "fsdp"), None),
            P(("dp", "fsdp"), None),
            P("fsdp", None),
            P(),
            P(),
            P(),
        ),
        check_vma=False,
    )
```
